512 devices in a mesh: panel: 16 (over x_lo, y, core), sc: 32 (over z, x_hi).
Axes of the slice: x: 4 (x_hi: 2, x_lo: 2; x = x_hi * 2 + x_lo), y: 4, z: 16, core: 2. Of those that a mesh axis runs over, the one named last changes fastest.
Arguments:
- captured_waveform: bfloat16 [16, 14, 1024, 4096], P(None, None, 'sc', 'panel'), may hold values from -6 to 6
- element_lookup: int32 [2048], P('panel'), may hold values from 0 to 2047, as said below
- combiner: bfloat16 [2048, 128], P('panel'), may hold values from -0.09375 to 0.09375
- pilot_syms: int32 [2], replicated, may hold values from 0 to 13
- pilot_values: float32 [2, 16384], P(None, ('panel', 'sc')), may hold values from -5 to 5
- mod_order: int32 [4096], P(('panel', 'sc')), may hold values from 1 to 4
- conv_first: bfloat16 [3, 3, 256, 128], replicated, may hold values from -0.1875 to 0.1875
- conv_rest: bfloat16 [5, 3, 3, 128, 128], replicated, may hold values from -0.25 to 0.25
- conv_bias: float32 [6, 128], replicated, may hold values from -1.5 to 1.5
- demap_in: bfloat16 [128, 256], replicated, may hold values from -0.75 to 0.75
- demap_bias: float32 [256], replicated, may hold values from -1.5 to 1.5
- demap_out: bfloat16 [256, 128], replicated, may hold values from -0.5 to 0.5
Outputs:
- llr: float32 [14, 16384, 128], P(None, ('panel', 'sc'))
The draws below stay inside these ranges and needn't reach their ends.
Inputs may be any that keep to these rules, and one draw needn't show every extreme that they name: `element_lookup`: the rows of each panel (blocks of 2048 // 16 rows) map to a permutation of that block's own indices.
All inputs are finite; a program needn't handle non-finite values.
Results may differ from the reference program's by a relative error of at most 0.035.
Values may be sent and summed in bfloat16 or wider, within the bound.
No kernel may reach another device: no remote copies, remote signals or barrier semaphores. Data moves between devices by JAX's collectives and lax.ppermute only.
A program may use at most 64 MiB of HBM per device.

```python
import jax
import jax.numpy as jnp
from jax import lax

RADIATOR_COUNT = 2048
LOBE_NUMBER = 64
FRAME_INTERVALS = 14
RB_SC = 4
PILOTS = 2
CH = 128
LAYERS = 6
HID = 256
STREAMS = 16
BITS = 8
TONE_BUNDLES = 16
BUNDLE_TONES = 1024
SC = 16384
N_PANEL = 16


def draw_element_lookup(key, part):
    key = jax.random.fold_in(key, 5)
    antennas_each_panel = RADIATOR_COUNT // N_PANEL
    panel_keys = jax.random.split(key, N_PANEL)
    permuted_rows = jax.vmap(lambda panel_key: jax.random.permutation(panel_key, antennas_each_panel))(panel_keys)
    start_positions = (jnp.arange(N_PANEL) * antennas_each_panel)[:, None]
    return (permuted_rows + start_positions).reshape(RADIATOR_COUNT).astype(jnp.int32)


def place_ends(entries, key, smallest, largest):
    index_at = [jax.random.randint(jax.random.fold_in(key, axis), (), 0, length) for axis, length in enumerate(entries.shape)]
    main_axis = entries.shape.index(max(entries.shape))
    neighbour = index_at[:main_axis] + [(index_at[main_axis] + 1) % entries.shape[main_axis]] + index_at[main_axis + 1:]
    return entries.at[tuple(index_at)].set(smallest).at[tuple(neighbour)].set(largest)


def level_of(own_key, extent, pieces, least, high):
    def one(axis_at, blocks):
        draws = jax.random.uniform(jax.random.fold_in(jax.random.fold_in(own_key, 6), axis_at), (blocks,), jnp.float32, least / len(pieces), high / len(pieces))
        return jnp.repeat(jnp.exp(draws), extent[axis_at] // blocks).reshape((-1,) + (1,) * (len(extent) - axis_at - 1))

    gain = one(*pieces[0])
    for cut in pieces[1:]:
        gain = gain * one(*cut)
    return gain


def bell_draw(rng, shape, scale, reach, shards=(), held_as=jnp.bfloat16):
    values = jax.random.normal(rng, shape, jnp.float32) * scale
    if len(shards) > 0:
        values = level_of(rng, shape, shards, -0.22, 0.18) * values
    return jnp.clip(values, min=-reach, max=reach).astype(held_as)


def setup_inputs(seed: int = 0) -> dict:
    arg_keys = jax.random.split(jax.random.key(seed), 13)
    return {
        "captured_waveform": bell_draw(arg_keys[0], (TONE_BUNDLES, FRAME_INTERVALS, BUNDLE_TONES, 2 * RADIATOR_COUNT), 1.0, 6.0, ((2, 32), (3, 16))),
        "element_lookup": draw_element_lookup(jax.random.fold_in(arg_keys[12], 71), 0),
        "combiner": bell_draw(arg_keys[2], (RADIATOR_COUNT, 2 * LOBE_NUMBER), (2 * RADIATOR_COUNT) ** -0.5, 0.09375, ((0, 16),)),
        "pilot_syms": jax.random.randint(arg_keys[3], (PILOTS,), 0, FRAME_INTERVALS).astype(jnp.int32),
        "pilot_values": bell_draw(arg_keys[4], (2, SC), 1.0, 5.0, ((1, 512),), jnp.float32),
        "mod_order": place_ends(jax.random.randint(arg_keys[5], (SC // RB_SC,), 1, 5), jax.random.fold_in(arg_keys[5], 1), 1, 4).astype(jnp.int32),
        "conv_first": bell_draw(arg_keys[6], (3, 3, 4 * LOBE_NUMBER, CH), (18 * LOBE_NUMBER) ** -0.5, 0.1875),
        "conv_rest": bell_draw(arg_keys[7], (LAYERS - 1, 3, 3, CH, CH), (9 * CH // 2) ** -0.5, 0.25),
        "conv_bias": bell_draw(arg_keys[8], (LAYERS, CH), 0.3, 1.5, (), jnp.float32),
        "demap_in": bell_draw(arg_keys[9], (CH, HID), (CH // 2) ** -0.5, 0.75),
        "demap_bias": bell_draw(arg_keys[10], (HID,), 0.3, 1.5, (), jnp.float32),
        "demap_out": bell_draw(arg_keys[11], (HID, STREAMS * BITS), (HID // 2) ** -0.5, 0.5),
    }


def build_matrix(combiner_rows):
    beam_count = combiner_rows.shape[1] // 2
    real_part = combiner_rows[:, :beam_count]
    imag_part = combiner_rows[:, beam_count:]
    real_row = jnp.concatenate([real_part, imag_part], 1)
    imag_row = jnp.concatenate([-imag_part, real_part], 1)
    return jnp.stack([real_row, imag_row], 1).reshape(2 * combiner_rows.shape[0], 2 * beam_count)


def convolve(field, kernel, layer_bias):
    sym_count, sub_count, channels = field.shape
    padded = jnp.pad(field, ((1, 1), (1, 1), (0, 0)))
    reduced_totals = jnp.zeros((sym_count * sub_count, kernel.shape[3]), jnp.float32)
    for shift_sym in range(3):
        for shift_sub in range(3):
            piece = padded[shift_sym:shift_sym + sym_count, shift_sub:shift_sub + sub_count].reshape(-1, channels)
            reduced_totals = reduced_totals + jnp.dot(piece, kernel[shift_sym, shift_sub], preferred_element_type=jnp.float32)
    result = jax.nn.relu(reduced_totals + layer_bias[None, :]).astype(jnp.bfloat16)
    return result.reshape(sym_count, sub_count, -1)


def reference(captured_waveform, element_lookup, combiner, pilot_syms, pilot_values, mod_order, conv_first, conv_rest, conv_bias, demap_in, demap_bias, demap_out):
    matrix = build_matrix(combiner[element_lookup])
    panel_span = 2 * RADIATOR_COUNT // N_PANEL
    unrolled_lines = N_PANEL * FRAME_INTERVALS * BUNDLE_TONES

    def add_panel(panel_idx, reduced_totals):
        offset = (panel_idx * panel_span).astype(jnp.int32)
        sample_block = lax.dynamic_slice_in_dim(captured_waveform, offset, panel_span, 3)
        matrix_rows = lax.dynamic_slice_in_dim(matrix, offset, panel_span, 0)
        panel_term = jnp.dot(sample_block.reshape(unrolled_lines, panel_span), matrix_rows, preferred_element_type=jnp.float32)
        rounded = lax.optimization_barrier(panel_term.astype(jnp.bfloat16))
        return reduced_totals + rounded.astype(jnp.float32)

    reduced_totals = lax.fori_loop(0, N_PANEL, add_panel, jnp.zeros((unrolled_lines, 2 * LOBE_NUMBER), jnp.float32))
    lobe_outputs = reduced_totals.astype(jnp.bfloat16).reshape(N_PANEL, FRAME_INTERVALS, BUNDLE_TONES, 2 * LOBE_NUMBER)
    lobe_outputs = lobe_outputs.transpose(1, 0, 2, 3).reshape(FRAME_INTERVALS, SC, 2 * LOBE_NUMBER)
    is_pilot = jnp.any(jnp.arange(FRAME_INTERVALS)[:, None] == pilot_syms[None, :], axis=1).astype(jnp.float32)
    beam_float = lobe_outputs.astype(jnp.float32)
    beam_re = beam_float[..., :LOBE_NUMBER]
    beam_im = beam_float[..., LOBE_NUMBER:]
    pilot_re = pilot_values[0][None, :, None]
    pilot_im = pilot_values[1][None, :, None]
    estimate = jnp.concatenate([beam_re * pilot_re + beam_im * pilot_im, beam_im * pilot_re - beam_re * pilot_im], -1)
    estimate = (estimate * is_pilot[:, None, None]).astype(jnp.bfloat16)
    field = jnp.concatenate([lobe_outputs, estimate], -1)
    for layer_idx in range(LAYERS):
        kernel = conv_first if layer_idx == 0 else conv_rest[layer_idx - 1]
        field = convolve(field, kernel, conv_bias[layer_idx])
    hidden = jnp.dot(field.reshape(FRAME_INTERVALS * SC, CH), demap_in, preferred_element_type=jnp.float32)
    hidden = jax.nn.relu(hidden + demap_bias[None, :]).astype(jnp.bfloat16)
    llr_values = jnp.dot(hidden, demap_out, preferred_element_type=jnp.float32).reshape(FRAME_INTERVALS, SC, STREAMS * BITS)
    bit_limit = 2 * jnp.repeat(mod_order, RB_SC)
    bit_index = jnp.arange(STREAMS * BITS) % BITS
    keep_mask = (bit_index[None, None, :] < bit_limit[None, :, None]) & (is_pilot[:, None, None] == 0.0)
    return jnp.where(keep_mask, llr_values, jnp.float32(0.0))
```

```python
import jax
import jax.numpy as jnp
from jax import lax
from jax.experimental import pallas as pl
from jax.experimental.pallas import tpu as pltpu
from jax.sharding import PartitionSpec as P

RB_SC = 4
BITS = 8
EDGE = 8
PANEL = "panel"
SUB = "sc"


def lookup_matrix(lookup, rows):
    n, c = rows.shape
    member = lax.broadcasted_iota(jnp.int32, (n, n), 0) == lookup % n
    picked = lax.dot_general(
        member.astype(jnp.bfloat16), rows, (((0,), (0,)), ((), ())), preferred_element_type=jnp.float32
    ).astype(jnp.bfloat16)
    doubled = (
        lax.broadcasted_iota(jnp.int32, (2 * n, n), 0) // 2 == lax.broadcasted_iota(jnp.int32, (2 * n, n), 1)
    )
    w = jnp.dot(doubled.astype(jnp.bfloat16), picked, preferred_element_type=jnp.float32)
    lane = lax.broadcasted_iota(jnp.int32, w.shape, 1)
    turned = pltpu.roll(w, c // 2, 1) * jnp.where(lane < c // 2, -1.0, 1.0)
    odd = lax.broadcasted_iota(jnp.int32, w.shape, 0) % 2 == 1
    return jnp.where(odd, turned, w).astype(jnp.bfloat16)


def partial_kernel(lookup_ref, rows_ref, wave_ref, out_ref, matrix_ref):
    @pl.when(pl.program_id(0) == 0)
    def _():
        matrix_ref[...] = lookup_matrix(lookup_ref[...], rows_ref[...])

    g, t, s, k = wave_ref.shape
    out_ref[...] = (
        jnp.dot(wave_ref[...].reshape(g * t * s, k), matrix_ref[...], preferred_element_type=jnp.float32)
        .astype(jnp.bfloat16)
        .reshape(out_ref.shape)
    )


def beam_partials(wave, lookup, rows, step):
    groups, syms, subs, k = wave.shape
    c = rows.shape[1]
    return pl.pallas_call(
        partial_kernel,
        grid=(groups // step,),
        in_specs=[
            pl.BlockSpec((1, lookup.shape[0]), lambda i: (0, 0)),
            pl.BlockSpec(rows.shape, lambda i: (0, 0)),
            pl.BlockSpec((step, syms, subs, k), lambda i: (i, 0, 0, 0)),
        ],
        out_specs=pl.BlockSpec((step, syms, subs, c), lambda i: (i, 0, 0, 0)),
        out_shape=jax.ShapeDtypeStruct((groups, syms, subs, c), jnp.bfloat16),
        scratch_shapes=[pltpu.VMEM((k, c), jnp.bfloat16)],
        compiler_params=pltpu.CompilerParams(vmem_limit_bytes=16 * 2**20),
        name="partials",
    )(lookup.reshape(1, -1), rows, wave)


def as_column(row, count):
    diagonal = lax.broadcasted_iota(jnp.int32, (count, count), 0) == lax.broadcasted_iota(
        jnp.int32, (count, count), 1
    )
    return jnp.sum(jnp.where(diagonal, jnp.broadcast_to(row, (count, count)), 0.0), axis=1, keepdims=True)


def estimate_of(beams, pilot_re, pilot_im):
    c = beams.shape[-1]
    return beams * pilot_re + pltpu.roll(beams, c // 2, beams.ndim - 1) * pilot_im


def signed_pilots(pilot_ref, c):
    s = pilot_ref.shape[1]
    re = jnp.broadcast_to(as_column(pilot_ref[0:1, :], s), (s, c))
    im = jnp.broadcast_to(as_column(pilot_ref[1:2, :], s), (s, c))
    lane = lax.broadcasted_iota(jnp.int32, (s, c), 1)
    return re, jnp.where(lane < c // 2, im, -im)


def sum_kernel(syms_ref, pilot_ref, parts_ref, own_ref, head_ref, tail_ref):
    panels, syms, subs, c = parts_ref.shape
    re, im = signed_pilots(pilot_ref, c)
    for t in range(syms):
        total = parts_ref[0, t].astype(jnp.float32)
        for p in range(1, panels):
            total = total + parts_ref[p, t].astype(jnp.float32)
        beams = total.astype(jnp.bfloat16)
        is_pilot = jnp.where((syms_ref[0] == t) | (syms_ref[1] == t), 1.0, 0.0)
        estimate = (estimate_of(beams.astype(jnp.float32), re, im) * is_pilot).astype(jnp.bfloat16)
        own_ref[t, :, :c] = beams
        own_ref[t, :, c:] = estimate
        head_ref[t, :, :c] = beams[:EDGE]
        head_ref[t, :, c:] = estimate[:EDGE]
        tail_ref[t, :, :c] = beams[subs - EDGE :]
        tail_ref[t, :, c:] = estimate[subs - EDGE :]


def sum_beams(parts, pilot_syms, pilot_values):
    _, syms, subs, c = parts.shape
    vmem = pl.BlockSpec(memory_space=pltpu.VMEM)
    return pl.pallas_call(
        sum_kernel,
        in_specs=[pl.BlockSpec(memory_space=pltpu.SMEM), vmem, vmem],
        out_specs=[vmem] * 3,
        out_shape=[
            jax.ShapeDtypeStruct((syms, subs, 2 * c), jnp.bfloat16),
            jax.ShapeDtypeStruct((syms, EDGE, 2 * c), jnp.bfloat16),
            jax.ShapeDtypeStruct((syms, EDGE, 2 * c), jnp.bfloat16),
        ],
        compiler_params=pltpu.CompilerParams(vmem_limit_bytes=16 * 2**20),
        name="sum_beams",
    )(pilot_syms, pilot_values, parts)


def receiver_kernel(
    ends_ref, syms_ref, order_ref, own_ref, left_ref, right_ref, first_ref, rest_ref, bias_ref,
    in_ref, in_bias_ref, out_w_ref, llr_ref, wide_ref, even_ref, odd_ref,
):
    syms, subs, feats = own_ref.shape
    layers = rest_ref.shape[0] + 1
    width = subs + 2 * EDGE
    rows = syms * width
    c = bias_ref.shape[1]
    skip = EDGE - layers

    def put(ref, whole, ch):
        for shift in range(3):
            moved = whole if shift == 0 else pltpu.roll(whole, rows - shift, 0)
            ref[width : width + rows, shift * ch : (shift + 1) * ch] = moved.astype(jnp.bfloat16)

    for ref in (wide_ref, even_ref, odd_ref):
        ref[0:width] = jnp.zeros((width, ref.shape[1]), jnp.bfloat16)
        ref[width + rows :] = jnp.zeros((width, ref.shape[1]), jnp.bfloat16)

    field = jnp.concatenate(
        [
            left_ref[...].astype(jnp.float32),
            own_ref[...].astype(jnp.float32),
            right_ref[...].astype(jnp.float32),
        ],
        axis=1,
    ).reshape(rows, feats)
    field = pltpu.roll(field, rows - skip, 0)
    put(wide_ref, field, feats)

    column = lax.broadcasted_iota(jnp.int32, (width, c), 0)
    src = wide_ref
    for layer in range(layers):
        kernel = first_ref[...] if layer == 0 else rest_ref[layer - 1]
        taps = jnp.concatenate([src[dt * width : dt * width + rows] for dt in range(3)], axis=1)
        total = jnp.dot(taps, kernel, preferred_element_type=jnp.float32)
        total = jnp.maximum(total + bias_ref[layer : layer + 1, :], 0.0)
        off = layers - 1 - layer
        inside = (column >= jnp.where(ends_ref[0] == 1, off, 0)) & (
            column < jnp.where(ends_ref[1] == 1, off + subs, width)
        )
        total = jnp.where(inside[None], total.reshape(syms, width, c), 0.0).reshape(rows, c)
        if layer < layers - 1:
            src = (even_ref, odd_ref)[layer % 2]
            put(src, total, c)

    final = total.astype(jnp.bfloat16).reshape(syms, width, c)[:, :subs].reshape(syms * subs, c)
    hidden = jnp.dot(final, in_ref[...], preferred_element_type=jnp.float32)
    hidden = jnp.maximum(hidden + in_bias_ref[...], 0.0).astype(jnp.bfloat16)
    llr = jnp.dot(hidden, out_w_ref[...], preferred_element_type=jnp.float32)
    bits = llr.shape[1]
    block = lax.broadcasted_iota(jnp.int32, (subs, bits), 0) // RB_SC
    limit = jnp.zeros((subs, bits), jnp.int32)
    for b in range(subs // RB_SC):
        limit = jnp.where(block == b, 2 * order_ref[b], limit)
    bit = lax.broadcasted_iota(jnp.int32, (subs, bits), 1) % BITS
    for t in range(syms):
        data = jnp.where((syms_ref[0] == t) | (syms_ref[1] == t), 0, 1)
        llr_ref[t] = jnp.where(bit < limit * data, llr[t * subs : (t + 1) * subs], 0.0)


def receive(ends, pilot_syms, mod_order, own, left, right, first, rest, bias, d_in, d_bias, d_out):
    syms, subs, feats = own.shape
    layers = bias.shape[0]
    c = bias.shape[1]
    width = subs + 2 * EDGE
    smem = pl.BlockSpec(memory_space=pltpu.SMEM)
    vmem = pl.BlockSpec(memory_space=pltpu.VMEM)
    padded = (syms + 2) * width
    return pl.pallas_call(
        receiver_kernel,
        in_specs=[smem] * 3 + [vmem] * 9,
        out_specs=vmem,
        out_shape=jax.ShapeDtypeStruct((syms, subs, d_out.shape[1]), jnp.float32),
        scratch_shapes=[
            pltpu.VMEM((padded, 3 * feats), jnp.bfloat16),
            pltpu.VMEM((padded, 3 * c), jnp.bfloat16),
            pltpu.VMEM((padded, 3 * c), jnp.bfloat16),
        ],
        compiler_params=pltpu.CompilerParams(vmem_limit_bytes=32 * 2**20),
        name="receiver",
    )(
        ends, pilot_syms, mod_order, own, left, right,
        first.reshape(9 * feats, c), rest.reshape(layers - 1, 9 * c, c), bias,
        d_in, d_bias.reshape(1, -1), d_out,
    )


def per_device(
    captured_waveform,
    element_lookup,
    combiner,
    pilot_syms,
    pilot_values,
    mod_order,
    conv_first,
    conv_rest,
    conv_bias,
    demap_in,
    demap_bias,
    demap_out,
):
    parts = beam_partials(captured_waveform, element_lookup, combiner, 2)
    parts = lax.all_to_all(parts, PANEL, 0, 0, tiled=True)
    own, head, tail = sum_beams(parts, pilot_syms, pilot_values)
    both = (PANEL, SUB)
    count = lax.axis_size(both)
    left = lax.ppermute(tail, both, [(i, i + 1) for i in range(count - 1)])
    right = lax.ppermute(head, both, [(i + 1, i) for i in range(count - 1)])
    at = lax.axis_index(both)
    ends = jnp.stack([at == 0, at == count - 1]).astype(jnp.int32)
    return receive(
        ends, pilot_syms, mod_order, own, left, right, conv_first, conv_rest, conv_bias,
        demap_in, demap_bias, demap_out,
    )


def solution(mesh):
    in_specs = (
        P(None, None, SUB, PANEL),
        P(PANEL),
        P(PANEL, None),
        P(),
        P(None, (PANEL, SUB)),
        P((PANEL, SUB)),
        P(),
        P(),
        P(),
        P(),
        P(),
        P(),
    )
    out_specs = P(None, (PANEL, SUB), None)
    return jax.shard_map(
        per_device, mesh=mesh, in_specs=in_specs, out_specs=out_specs, check_vma=False
    )
```

```python
import jax
import jax.numpy as jnp
from jax import lax
from jax.experimental import pallas as pl
from jax.experimental.pallas import tpu as pltpu
from jax.sharding import PartitionSpec as P

RB_SC = 4
BITS = 8
PILOTS = 2
EDGE = 8
PANEL = "panel"
SUB = "sc"


def lookup_matrix(lookup, rows):
    n, c = rows.shape
    member = lax.broadcasted_iota(jnp.int32, (n, n), 0) == lookup % n
    picked = lax.dot_general(
        member.astype(jnp.bfloat16), rows, (((0,), (0,)), ((), ())), preferred_element_type=jnp.float32
    ).astype(jnp.bfloat16)
    doubled = (
        lax.broadcasted_iota(jnp.int32, (2 * n, n), 0) // 2 == lax.broadcasted_iota(jnp.int32, (2 * n, n), 1)
    )
    w = jnp.dot(doubled.astype(jnp.bfloat16), picked, preferred_element_type=jnp.float32)
    lane = lax.broadcasted_iota(jnp.int32, w.shape, 1)
    turned = pltpu.roll(w, c // 2, 1) * jnp.where(lane < c // 2, -1.0, 1.0)
    odd = lax.broadcasted_iota(jnp.int32, w.shape, 0) % 2 == 1
    return jnp.where(odd, turned, w).astype(jnp.bfloat16)


def matrix_kernel_body(wave_ref, out_ref, blocks_ref, sems, matrix, parity):
    count, syms, subs, c = out_ref.shape
    k = wave_ref.shape[3]

    def fetch(i):
        return pltpu.make_async_copy(wave_ref.at[2 * i + parity], blocks_ref.at[i], sems.at[i])

    for i in range(count):
        fetch(i).start()
    weights = matrix()
    for i in range(count):
        fetch(i).wait()
        out_ref[i] = (
            jnp.dot(blocks_ref[i].reshape(syms * subs, k), weights, preferred_element_type=jnp.float32)
            .astype(jnp.bfloat16)
            .reshape(syms, subs, c)
        )


def given_kernel(lookup_ref, rows_ref, wave_ref, out_ref, matrix_ref, blocks_ref, lookup_buf, rows_buf, sems):
    count = out_ref.shape[0]
    copies = [
        pltpu.make_async_copy(lookup_ref, lookup_buf, sems.at[count]),
        pltpu.make_async_copy(rows_ref, rows_buf, sems.at[count + 1]),
    ]
    for copy in copies:
        copy.start()

    def matrix():
        for copy in copies:
            copy.wait()
        matrix_ref[...] = lookup_matrix(lookup_buf[...], rows_buf[...])
        return matrix_ref[...]

    parity = 1 - lax.axis_index(PANEL) % 2
    matrix_kernel_body(wave_ref, out_ref, blocks_ref, sems, matrix, parity)


def kept_kernel(matrix_ref, wave_ref, out_ref, blocks_ref, sems):
    parity = lax.axis_index(PANEL) % 2
    matrix_kernel_body(wave_ref, out_ref, blocks_ref, sems, lambda: matrix_ref[...], parity)


def beam_partials(wave, lookup, rows):
    groups, syms, subs, k = wave.shape
    n, c = rows.shape
    half = groups // 2
    lookup, rows, wave = (
        pltpu.with_memory_space_constraint(array, pltpu.HBM) for array in (lookup.reshape(1, -1), rows, wave)
    )
    hbm = pl.BlockSpec(memory_space=pltpu.HBM)
    vmem = pl.BlockSpec(memory_space=pltpu.VMEM)
    params = pltpu.CompilerParams(vmem_limit_bytes=8 * 2**20)
    out = jax.ShapeDtypeStruct((half, syms, subs, c), jnp.bfloat16)
    blocks = pltpu.VMEM((half, syms, subs, k), jnp.bfloat16)
    given, matrix = pl.pallas_call(
        given_kernel,
        in_specs=[hbm] * 3,
        out_specs=[vmem] * 2,
        out_shape=[out, jax.ShapeDtypeStruct((k, c), jnp.bfloat16)],
        scratch_shapes=[
            blocks,
            pltpu.VMEM((1, n), jnp.int32),
            pltpu.VMEM((n, c), jnp.bfloat16),
            pltpu.SemaphoreType.DMA((half + 2,)),
        ],
        compiler_params=params,
        name="given",
    )(lookup, rows, wave)
    kept = pl.pallas_call(
        kept_kernel,
        in_specs=[vmem, hbm],
        out_specs=vmem,
        out_shape=out,
        scratch_shapes=[blocks, pltpu.SemaphoreType.DMA((half,))],
        compiler_params=params,
        cost_estimate=pl.CostEstimate(
            flops=2 * half * syms * subs * k * c, bytes_accessed=2 * half * syms * subs * k, transcendentals=0
        ),
        name="kept",
    )(matrix, wave)
    return given, kept


def as_column(row, count):
    diagonal = lax.broadcasted_iota(jnp.int32, (count, count), 0) == lax.broadcasted_iota(
        jnp.int32, (count, count), 1
    )
    return jnp.sum(jnp.where(diagonal, jnp.broadcast_to(row, (count, count)), 0.0), axis=1, keepdims=True)


def estimate_of(beams, pilot_re, pilot_im):
    c = beams.shape[-1]
    return beams * pilot_re + pltpu.roll(beams, c // 2, beams.ndim - 1) * pilot_im


def signed_pilots(pilot_ref, c):
    s = pilot_ref.shape[1]
    re = jnp.broadcast_to(as_column(pilot_ref[0:1, :], s), (s, c))
    im = jnp.broadcast_to(as_column(pilot_ref[1:2, :], s), (s, c))
    lane = lax.broadcasted_iota(jnp.int32, (s, c), 1)
    return re, jnp.where(lane < c // 2, im, -im)


def sum_kernel(syms_ref, pilot_ref, parts_ref, own_ref, head_ref, tail_ref):
    panels, syms, subs, c = parts_ref.shape
    for t in range(syms):
        total = parts_ref[0, t].astype(jnp.float32)
        for p in range(1, panels):
            total = total + parts_ref[p, t].astype(jnp.float32)
        beams = total.astype(jnp.bfloat16)
        own_ref[t] = beams
        head_ref[t] = beams[:EDGE]
        tail_ref[t] = beams[subs - EDGE :]
    re, im = signed_pilots(pilot_ref, c)
    for i in range(PILOTS):
        at_pilot = own_ref[syms_ref[i]].astype(jnp.float32)
        estimate = estimate_of(at_pilot, re, im).astype(jnp.bfloat16)
        own_ref[syms + i] = estimate
        head_ref[syms + i] = estimate[:EDGE]
        tail_ref[syms + i] = estimate[subs - EDGE :]


def sum_beams(parts, pilot_syms, pilot_values):
    _, syms, subs, c = parts.shape
    vmem = pl.BlockSpec(memory_space=pltpu.VMEM)
    return pl.pallas_call(
        sum_kernel,
        in_specs=[pl.BlockSpec(memory_space=pltpu.SMEM), vmem, vmem],
        out_specs=[vmem] * 3,
        out_shape=[
            jax.ShapeDtypeStruct((syms + PILOTS, subs, c), jnp.bfloat16),
            jax.ShapeDtypeStruct((syms + PILOTS, EDGE, c), jnp.bfloat16),
            jax.ShapeDtypeStruct((syms + PILOTS, EDGE, c), jnp.bfloat16),
        ],
        compiler_params=pltpu.CompilerParams(vmem_limit_bytes=8 * 2**20),
        name="sum_beams",
    )(pilot_syms, pilot_values, parts)


def receiver_kernel(
    ends_ref, syms_ref, order_ref, own_ref, left_ref, right_ref, first_ref, rest_ref, bias_ref,
    in_ref, in_bias_ref, out_w_ref, llr_ref, wide_ref, even_ref, odd_ref,
):
    syms, subs, c = own_ref.shape
    syms, feats = syms - PILOTS, 2 * c
    layers = rest_ref.shape[0] + 1
    width = subs + 2 * EDGE
    rows = syms * width
    skip = EDGE - layers

    def put(ref, whole, ch):
        for shift in range(3):
            moved = whole if shift == 0 else pltpu.roll(whole, rows - shift, 0)
            ref[width : width + rows, shift * ch : (shift + 1) * ch] = moved.astype(jnp.bfloat16)

    for ref in (wide_ref, even_ref, odd_ref):
        ref[0:width] = jnp.zeros((width, ref.shape[1]), jnp.bfloat16)
        ref[width + rows :] = jnp.zeros((width, ref.shape[1]), jnp.bfloat16)

    pieces = jnp.concatenate(
        [
            left_ref[...].astype(jnp.float32),
            own_ref[...].astype(jnp.float32),
            right_ref[...].astype(jnp.float32),
        ],
        axis=1,
    )
    estimates = []
    for t in range(syms):
        estimate = jnp.zeros((width, c), jnp.float32)
        for i in range(PILOTS):
            estimate = jnp.where(syms_ref[i] == t, pieces[syms + i], estimate)
        estimates.append(estimate)
    field = jnp.concatenate([pieces[:syms], jnp.stack(estimates, 0)], axis=2).reshape(rows, feats)
    field = pltpu.roll(field, rows - skip, 0)
    put(wide_ref, field, feats)

    column = lax.broadcasted_iota(jnp.int32, (width, c), 0)
    src = wide_ref
    for layer in range(layers):
        kernel = first_ref[...] if layer == 0 else rest_ref[layer - 1]
        taps = jnp.concatenate([src[dt * width : dt * width + rows] for dt in range(3)], axis=1)
        total = jnp.dot(taps, kernel, preferred_element_type=jnp.float32)
        total = jnp.maximum(total + bias_ref[layer : layer + 1, :], 0.0)
        off = layers - 1 - layer
        inside = (column >= jnp.where(ends_ref[0] == 1, off, 0)) & (
            column < jnp.where(ends_ref[1] == 1, off + subs, width)
        )
        total = jnp.where(inside[None], total.reshape(syms, width, c), 0.0).reshape(rows, c)
        if layer < layers - 1:
            src = (even_ref, odd_ref)[layer % 2]
            put(src, total, c)

    final = total.astype(jnp.bfloat16).reshape(syms, width, c)[:, :subs].reshape(syms * subs, c)
    hidden = jnp.dot(final, in_ref[...], preferred_element_type=jnp.float32)
    hidden = jnp.maximum(hidden + in_bias_ref[...], 0.0).astype(jnp.bfloat16)
    llr = jnp.dot(hidden, out_w_ref[...], preferred_element_type=jnp.float32)
    bits = llr.shape[1]
    block = lax.broadcasted_iota(jnp.int32, (subs, bits), 0) // RB_SC
    limit = jnp.zeros((subs, bits), jnp.int32)
    for b in range(subs // RB_SC):
        limit = jnp.where(block == b, 2 * order_ref[b], limit)
    bit = lax.broadcasted_iota(jnp.int32, (subs, bits), 1) % BITS
    for t in range(syms):
        data = jnp.where((syms_ref[0] == t) | (syms_ref[1] == t), 0, 1)
        llr_ref[t] = jnp.where(bit < limit * data, llr[t * subs : (t + 1) * subs], 0.0)


def receive(ends, pilot_syms, mod_order, own, left, right, first, rest, bias, d_in, d_bias, d_out):
    syms, subs, c = own.shape
    syms, feats = syms - PILOTS, 2 * c
    layers = bias.shape[0]
    width = subs + 2 * EDGE
    smem = pl.BlockSpec(memory_space=pltpu.SMEM)
    vmem = pl.BlockSpec(memory_space=pltpu.VMEM)
    padded = (syms + 2) * width
    return pl.pallas_call(
        receiver_kernel,
        in_specs=[smem] * 3 + [vmem] * 9,
        out_specs=vmem,
        out_shape=jax.ShapeDtypeStruct((syms, subs, d_out.shape[1]), jnp.float32),
        scratch_shapes=[
            pltpu.VMEM((padded, 3 * feats), jnp.bfloat16),
            pltpu.VMEM((padded, 3 * c), jnp.bfloat16),
            pltpu.VMEM((padded, 3 * c), jnp.bfloat16),
        ],
        compiler_params=pltpu.CompilerParams(vmem_limit_bytes=32 * 2**20),
        name="receiver",
    )(
        ends, pilot_syms, mod_order, own, left, right,
        first.reshape(9 * feats, c), rest.reshape(layers - 1, 9 * c, c), bias,
        d_in, d_bias.reshape(1, -1), d_out,
    )


def per_device(
    captured_waveform,
    element_lookup,
    combiner,
    pilot_syms,
    pilot_values,
    mod_order,
    conv_first,
    conv_rest,
    conv_bias,
    demap_in,
    demap_bias,
    demap_out,
):
    given, kept = beam_partials(captured_waveform, element_lookup, combiner)
    panels = lax.axis_size(PANEL)
    got = lax.ppermute(given, PANEL, [(p, p ^ 1) for p in range(panels)])
    pairs = (kept.astype(jnp.float32) + got.astype(jnp.float32)).astype(jnp.bfloat16)
    same_core = [list(range(core, panels, 2)) for core in range(2)]
    parts = lax.all_to_all(pairs, PANEL, 0, 0, axis_index_groups=same_core, tiled=True)
    own, head, tail = sum_beams(parts, pilot_syms, pilot_values)
    both = (PANEL, SUB)
    count = lax.axis_size(both)
    left = lax.ppermute(tail, both, [(i, i + 1) for i in range(count - 1)])
    right = lax.ppermute(head, both, [(i + 1, i) for i in range(count - 1)])
    at = lax.axis_index(both)
    ends = jnp.stack([at == 0, at == count - 1]).astype(jnp.int32)
    return receive(
        ends, pilot_syms, mod_order, own, left, right, conv_first, conv_rest, conv_bias,
        demap_in, demap_bias, demap_out,
    )


def solution(mesh):
    in_specs = (
        P(None, None, SUB, PANEL),
        P(PANEL),
        P(PANEL, None),
        P(),
        P(None, (PANEL, SUB)),
        P((PANEL, SUB)),
        P(),
        P(),
        P(),
        P(),
        P(),
        P(),
    )
    out_specs = P(None, (PANEL, SUB), None)
    return jax.shard_map(
        per_device, mesh=mesh, in_specs=in_specs, out_specs=out_specs, check_vma=False
    )
```

```python
import jax
import jax.numpy as jnp
from jax import lax
from jax.experimental import pallas as pl
from jax.experimental.pallas import tpu as pltpu
from jax.sharding import PartitionSpec as P

RB_SC = 4
BITS = 8
PILOTS = 2
EDGE = 8
PANEL = "panel"
SUB = "sc"


def lookup_matrix(lookup, rows):
    n, c = rows.shape
    member = lax.broadcasted_iota(jnp.int32, (n, n), 0) == lookup % n
    picked = lax.dot_general(
        member.astype(jnp.bfloat16), rows, (((0,), (0,)), ((), ())), preferred_element_type=jnp.float32
    ).astype(jnp.bfloat16)
    doubled = (
        lax.broadcasted_iota(jnp.int32, (2 * n, n), 0) // 2 == lax.broadcasted_iota(jnp.int32, (2 * n, n), 1)
    )
    w = jnp.dot(doubled.astype(jnp.bfloat16), picked, preferred_element_type=jnp.float32)
    lane = lax.broadcasted_iota(jnp.int32, w.shape, 1)
    turned = pltpu.roll(w, c // 2, 1) * jnp.where(lane < c // 2, -1.0, 1.0)
    odd = lax.broadcasted_iota(jnp.int32, w.shape, 0) % 2 == 1
    return jnp.where(odd, turned, w).astype(jnp.bfloat16)


def matrix_kernel_body(wave_ref, out_ref, blocks_ref, sems, matrix, parity):
    count, syms, subs, c = out_ref.shape
    k = wave_ref.shape[3]

    def fetch(i):
        return pltpu.make_async_copy(wave_ref.at[2 * i + parity], blocks_ref.at[i], sems.at[i])

    for i in range(count):
        fetch(i).start()
    weights = matrix()
    for first, last in ((0, count // 4), (count // 4, count)):
        for i in range(first, last):
            fetch(i).wait()
        lines = blocks_ref[first:last].reshape((last - first) * syms * subs, k)
        out_ref[first:last] = (
            jnp.dot(lines, weights, preferred_element_type=jnp.float32)
            .astype(jnp.bfloat16)
            .reshape(last - first, syms, subs, c)
        )


def given_kernel(lookup_ref, rows_ref, wave_ref, out_ref, matrix_ref, blocks_ref, lookup_buf, rows_buf, sems):
    count = out_ref.shape[0]
    copies = [
        pltpu.make_async_copy(lookup_ref, lookup_buf, sems.at[count]),
        pltpu.make_async_copy(rows_ref, rows_buf, sems.at[count + 1]),
    ]
    for copy in copies:
        copy.start()

    def matrix():
        for copy in copies:
            copy.wait()
        matrix_ref[...] = lookup_matrix(lookup_buf[...], rows_buf[...])
        return matrix_ref[...]

    parity = 1 - lax.axis_index(PANEL) % 2
    matrix_kernel_body(wave_ref, out_ref, blocks_ref, sems, matrix, parity)


def kept_kernel(matrix_ref, wave_ref, out_ref, blocks_ref, sems):
    parity = lax.axis_index(PANEL) % 2
    matrix_kernel_body(wave_ref, out_ref, blocks_ref, sems, lambda: matrix_ref[...], parity)


def beam_partials(wave, lookup, rows):
    groups, syms, subs, k = wave.shape
    n, c = rows.shape
    half = groups // 2
    lookup, rows, wave = (
        pltpu.with_memory_space_constraint(array, pltpu.HBM) for array in (lookup.reshape(1, -1), rows, wave)
    )
    hbm = pl.BlockSpec(memory_space=pltpu.HBM)
    vmem = pl.BlockSpec(memory_space=pltpu.VMEM)
    params = pltpu.CompilerParams(vmem_limit_bytes=8 * 2**20)
    out = jax.ShapeDtypeStruct((half, syms, subs, c), jnp.bfloat16)
    blocks = pltpu.VMEM((half, syms, subs, k), jnp.bfloat16)
    given, matrix = pl.pallas_call(
        given_kernel,
        in_specs=[hbm] * 3,
        out_specs=[vmem] * 2,
        out_shape=[out, jax.ShapeDtypeStruct((k, c), jnp.bfloat16)],
        scratch_shapes=[
            blocks,
            pltpu.VMEM((1, n), jnp.int32),
            pltpu.VMEM((n, c), jnp.bfloat16),
            pltpu.SemaphoreType.DMA((half + 2,)),
        ],
        compiler_params=params,
        name="given",
    )(lookup, rows, wave)
    kept = pl.pallas_call(
        kept_kernel,
        in_specs=[vmem, hbm],
        out_specs=vmem,
        out_shape=out,
        scratch_shapes=[blocks, pltpu.SemaphoreType.DMA((half,))],
        compiler_params=params,
        cost_estimate=pl.CostEstimate(
            flops=2 * half * syms * subs * k * c, bytes_accessed=2 * half * syms * subs * k, transcendentals=0
        ),
        name="kept",
    )(matrix, wave)
    return given, kept


def as_column(row, count):
    diagonal = lax.broadcasted_iota(jnp.int32, (count, count), 0) == lax.broadcasted_iota(
        jnp.int32, (count, count), 1
    )
    return jnp.sum(jnp.where(diagonal, jnp.broadcast_to(row, (count, count)), 0.0), axis=1, keepdims=True)


def estimate_of(beams, pilot_re, pilot_im):
    c = beams.shape[-1]
    return beams * pilot_re + pltpu.roll(beams, c // 2, beams.ndim - 1) * pilot_im


def signed_pilots(pilot_ref, c):
    s = pilot_ref.shape[1]
    re = jnp.broadcast_to(as_column(pilot_ref[0:1, :], s), (s, c))
    im = jnp.broadcast_to(as_column(pilot_ref[1:2, :], s), (s, c))
    lane = lax.broadcasted_iota(jnp.int32, (s, c), 1)
    return re, jnp.where(lane < c // 2, im, -im)


def position():
    blocks = lax.axis_size(SUB)
    return lax.axis_index(PANEL) * blocks + lax.axis_index(SUB), lax.axis_size(PANEL) * blocks


def first_half(rows, low, high):
    return jnp.where(lax.broadcasted_iota(jnp.int32, rows, len(rows) - 2) < EDGE // 2, low, high)


def sum_kernel(syms_ref, pilot_ref, parts_ref, own_ref, first_ref, second_ref, beams_ref):
    panels, syms, subs, c = parts_ref.shape
    for t in range(syms):
        total = parts_ref[0, t].astype(jnp.float32)
        for p in range(1, panels):
            total = total + parts_ref[p, t].astype(jnp.float32)
        beams_ref[t] = total.astype(jnp.bfloat16).astype(jnp.float32)
    re, im = signed_pilots(pilot_ref, c)
    for i in range(PILOTS):
        beams_ref[syms + i] = estimate_of(beams_ref[syms_ref[i]], re, im)
    half = EDGE // 2
    even = beams_ref[:, pl.ds(0, subs // 2, 2), :]
    odd = beams_ref[:, pl.ds(1, subs // 2, 2), :]
    own_ref[:, :, :c] = even.astype(jnp.bfloat16)
    own_ref[:, :, c:] = odd.astype(jnp.bfloat16)
    rows = (syms + PILOTS, EDGE, c)
    head = first_half(rows, even[:, :EDGE], pltpu.roll(odd[:, :EDGE], half, 1))
    tail = first_half(rows, pltpu.roll(even[:, subs // 2 - EDGE :], half, 1), odd[:, subs // 2 - EDGE :])
    to_right = position()[0] % 2 == 0
    first_ref[...] = jnp.where(to_right, tail, head).astype(jnp.bfloat16)
    second_ref[...] = jnp.where(to_right, head, tail).astype(jnp.bfloat16)


def sum_beams(parts, pilot_syms, pilot_values):
    _, syms, subs, c = parts.shape
    vmem = pl.BlockSpec(memory_space=pltpu.VMEM)
    edge = jax.ShapeDtypeStruct((syms + PILOTS, EDGE, c), jnp.bfloat16)
    return pl.pallas_call(
        sum_kernel,
        in_specs=[pl.BlockSpec(memory_space=pltpu.SMEM), vmem, vmem],
        out_specs=[vmem] * 3,
        out_shape=[jax.ShapeDtypeStruct((syms + PILOTS, subs // 2, 2 * c), jnp.bfloat16), edge, edge],
        scratch_shapes=[pltpu.VMEM((syms + PILOTS, subs, c), jnp.float32)],
        compiler_params=pltpu.CompilerParams(vmem_limit_bytes=8 * 2**20),
        name="sum_beams",
    )(pilot_syms, pilot_values, parts)


def pilot_rows(syms_ref, rows, syms):
    spread = []
    for t in range(syms):
        row = jnp.zeros(rows.shape[1:], rows.dtype)
        for i in range(PILOTS):
            row = jnp.where(syms_ref[i] == t, rows[i], row)
        spread.append(row)
    return jnp.stack(spread, 0)


def with_estimates(syms_ref, pairs, syms):
    c = pairs.shape[2] // 2
    beams, estimates = pairs[:syms], pilot_rows(syms_ref, pairs[syms:], syms)
    return jnp.concatenate([beams[..., :c], estimates[..., :c], beams[..., c:], estimates[..., c:]], axis=2)


def layer_sums(taps, kernel, bias):
    depth = kernel.shape[0] // 3
    zeros = jnp.zeros((depth // 3, kernel.shape[1]), kernel.dtype)
    total = jnp.concatenate([bias, bias], axis=1)
    for dt in range(3):
        part = kernel[dt * depth : (dt + 1) * depth]
        wide = jnp.concatenate(
            [jnp.concatenate([part, zeros], axis=0), jnp.concatenate([zeros, part], axis=0)], axis=1
        )
        total = total + jnp.dot(taps(dt), wide, preferred_element_type=jnp.float32)
    return jnp.maximum(total, 0.0)


def demapped(pairs, in_ref, in_bias_ref, out_w_ref):
    rows, c = pairs.shape[0], pairs.shape[1] // 2
    field = jnp.concatenate([pairs[:, :c], pairs[:, c:]], axis=0)
    hidden = jnp.dot(field, in_ref[...], preferred_element_type=jnp.float32)
    hidden = jnp.maximum(hidden + in_bias_ref[...], 0.0).astype(jnp.bfloat16)
    llr = jnp.dot(hidden, out_w_ref[...], preferred_element_type=jnp.float32)
    return llr[:rows], llr[rows:]


def bit_limits(order_ref, pairs, bits):
    row = lax.broadcasted_iota(jnp.int32, (len(pairs), bits), 0)
    limit = jnp.zeros((len(pairs), bits), jnp.int32)
    for block in sorted({2 * pair // RB_SC for pair in pairs}):
        at = [r for r, pair in enumerate(pairs) if 2 * pair // RB_SC == block]
        limit = jnp.where((row >= at[0]) & (row <= at[-1]), 2 * order_ref[block], limit)
    return limit


def store_llr(ref, llrs, limit, syms_ref):
    rows = limit.shape[0]
    bit = lax.broadcasted_iota(jnp.int32, limit.shape, 1) % BITS
    for t in range(ref.shape[0]):
        data = jnp.where((syms_ref[0] == t) | (syms_ref[1] == t), 0, 1)
        keep = bit < limit * data
        for side, llr in enumerate(llrs):
            ref[t, pl.ds(side, rows, 2), :] = jnp.where(keep, llr[t * rows : (t + 1) * rows], 0.0)


def interior_kernel(
    syms_ref, order_ref, own_ref, first_ref, rest_ref, bias_ref, in_ref, in_bias_ref, out_w_ref,
    llr_ref, patch_ref, wide_ref, even_ref, odd_ref,
):
    syms, pairs, c2 = own_ref.shape
    syms = syms - PILOTS
    layers = rest_ref.shape[0] + 1
    rows = syms * pairs
    for ref in (wide_ref, even_ref, odd_ref):
        ref[0:pairs] = jnp.zeros((pairs, ref.shape[1]), jnp.bfloat16)
        ref[pairs + rows :] = jnp.zeros((pairs, ref.shape[1]), jnp.bfloat16)

    def put(ref, whole):
        lanes = whole.shape[1]
        ref[pairs : pairs + rows, :lanes] = whole.astype(jnp.bfloat16)
        ref[pairs : pairs + rows, lanes:] = pltpu.roll(whole, rows - 1, 0).astype(jnp.bfloat16)

    field = with_estimates(syms_ref, own_ref[...].astype(jnp.float32), syms)
    put(wide_ref, field.reshape(rows, 2 * c2))
    src = wide_ref
    for layer in range(1, layers + 1):
        kernel = first_ref[...] if layer == 1 else rest_ref[layer - 2]
        total = layer_sums(
            lambda dt, src=src: src[dt * pairs : dt * pairs + rows], kernel, bias_ref[layer - 1 : layer, :]
        )
        if layer == layers:
            break
        src = (even_ref, odd_ref)[layer % 2]
        put(src, total)
        spread = total.reshape(syms, pairs, c2)
        last = pairs - 2 - layer
        group = last // 8 * 8
        low = pltpu.roll(spread[:, :8], 2, 1)
        high = spread[:, group : group + 8]
        if last % 8 != 4:
            high = pltpu.roll(high, (4 - last % 8) % 8, 1)
        patch_ref[layer - 1] = first_half((syms, 8, c2), low, high)
    final = pltpu.roll(total, layers // 2, 0).astype(jnp.bfloat16)
    llrs = demapped(final, in_ref, in_bias_ref, out_w_ref)
    store_llr(llr_ref, llrs, bit_limits(order_ref, list(range(pairs)), llr_ref.shape[2]), syms_ref)


def edge_kernel(
    syms_ref, order_ref, got_first_ref, got_second_ref, sent_first_ref, sent_second_ref, patch_ref, inner_ref,
    first_ref, rest_ref, bias_ref, in_ref, in_bias_ref, out_w_ref,
    llr_ref, llr_buf, sems,
):
    syms, half = got_first_ref.shape[0] - PILOTS, EDGE // 2
    layers = rest_ref.shape[0] + 1
    subs = llr_ref.shape[1]
    c2 = 2 * got_first_ref.shape[2]
    rows = syms * EDGE
    middle = pl.ds(EDGE, subs - 2 * EDGE)
    inner_copy = pltpu.make_async_copy(inner_ref.at[:, middle], llr_ref.at[:, middle], sems.at[2])
    inner_copy.start()

    def paired(ref_even, ref_odd):
        columns = jnp.where(to_right, ref_even[...], ref_odd[...]).astype(jnp.float32)
        return jnp.concatenate([columns, pltpu.roll(columns, half, 1)], axis=2)

    def row_of(shape):
        return lax.broadcasted_iota(jnp.int32, shape, len(shape) - 2)

    def convolved(this, after, kernel, bias):
        both = jnp.concatenate([this, after], axis=2)
        lanes = both.shape[2]
        padding = jnp.zeros((1, EDGE, lanes), jnp.float32)
        padded = jnp.concatenate([padding, both, padding], axis=0)
        return layer_sums(
            lambda dt: padded[dt : dt + syms].reshape(rows, lanes).astype(jnp.bfloat16), kernel, bias
        ).reshape(syms, EDGE, c2)

    at, blocks = position()
    to_right = at % 2 == 0
    left, right = paired(got_second_ref, got_first_ref), paired(got_first_ref, got_second_ref)
    tail, head = paired(sent_first_ref, sent_second_ref), paired(sent_second_ref, sent_first_ref)
    low = first_half(left.shape, left, pltpu.roll(head, half, 1))
    high = first_half(left.shape, tail, pltpu.roll(right, half, 1))
    this = first_half(low.shape, pltpu.roll(low, EDGE - 1, 1), pltpu.roll(high, 2, 1))
    after = first_half(low.shape, pltpu.roll(low, EDGE - 2, 1), pltpu.roll(high, 1, 1))
    total = convolved(
        with_estimates(syms_ref, this, syms), with_estimates(syms_ref, after, syms),
        first_ref[...], bias_ref[0:1, :],
    )
    row = row_of((EDGE, c2))
    odd = lax.broadcasted_iota(jnp.int32, (EDGE, c2), 1) // (c2 // 2)
    for layer in range(1, layers):
        below = (row < half) & (2 * row + odd < layers - layer) & (at == 0)
        above = (row >= half) & (2 * (row - half) + odd >= 2 + layer) & (at == blocks - 1)
        total = jnp.where((below | above)[None], 0.0, total)
        patch = patch_ref[layer - 1]
        rows_of = row_of(total.shape)
        this = jnp.where(rows_of < half, total, jnp.where(rows_of == half, patch, pltpu.roll(total, 1, 1)))
        after = jnp.where(
            rows_of < half - 1, pltpu.roll(total, EDGE - 1, 1), jnp.where(rows_of == half - 1, patch, total)
        )
        total = convolved(this, after, rest_ref[layer - 1], bias_ref[layer : layer + 1, :])
    llrs = demapped(total.reshape(rows, c2).astype(jnp.bfloat16), in_ref, in_bias_ref, out_w_ref)
    columns = [*range(half), *range(subs // 2 - half, subs // 2)]
    store_llr(llr_buf, llrs, bit_limits(order_ref, columns, llr_ref.shape[2]), syms_ref)
    copies = [
        pltpu.make_async_copy(
            llr_buf.at[:, pl.ds(side * EDGE, EDGE)], llr_ref.at[:, pl.ds(start, EDGE)], sems.at[side]
        )
        for side, start in enumerate((0, subs - EDGE))
    ]
    for copy in copies:
        copy.start()
    inner_copy.wait()
    for copy in copies:
        copy.wait()


def receive_interior(pilot_syms, mod_order, own, weights):
    syms, pairs, c2 = own.shape
    syms = syms - PILOTS
    bits = weights[-1].shape[1]
    layers = weights[1].shape[0] + 1
    smem = pl.BlockSpec(memory_space=pltpu.SMEM)
    vmem = pl.BlockSpec(memory_space=pltpu.VMEM)
    padded = (syms + 2) * pairs
    return pl.pallas_call(
        interior_kernel,
        in_specs=[smem] * 2 + [vmem] * 7,
        out_specs=[vmem] * 2,
        out_shape=[
            jax.ShapeDtypeStruct((syms, 2 * pairs, bits), jnp.float32),
            jax.ShapeDtypeStruct((layers - 1, syms, EDGE, c2), jnp.float32),
        ],
        scratch_shapes=[
            pltpu.VMEM((padded, 4 * c2), jnp.bfloat16),
            pltpu.VMEM((padded, 2 * c2), jnp.bfloat16),
            pltpu.VMEM((padded, 2 * c2), jnp.bfloat16),
        ],
        compiler_params=pltpu.CompilerParams(vmem_limit_bytes=16 * 2**20),
        cost_estimate=pl.CostEstimate(flops=10**9, bytes_accessed=4 * 10**6, transcendentals=0),
        name="interior",
    )(pilot_syms, mod_order, own, *weights)


def receive_edges(pilot_syms, mod_order, got, sent, patch, weights, inner):
    syms, subs, bits = inner.shape
    smem = pl.BlockSpec(memory_space=pltpu.SMEM)
    vmem = pl.BlockSpec(memory_space=pltpu.VMEM)
    return pl.pallas_call(
        edge_kernel,
        in_specs=[smem] * 2 + [vmem] * 12,
        out_specs=pl.BlockSpec(memory_space=pltpu.HBM),
        out_shape=pltpu.HBM(inner.shape, jnp.float32),
        scratch_shapes=[
            pltpu.VMEM((syms, 2 * EDGE, bits), jnp.float32),
            pltpu.SemaphoreType.DMA((3,)),
        ],
        compiler_params=pltpu.CompilerParams(vmem_limit_bytes=16 * 2**20),
        cost_estimate=pl.CostEstimate(flops=5 * 10**8, bytes_accessed=4 * 10**6, transcendentals=0),
        name="edges",
    )(pilot_syms, mod_order, *got, *sent, patch, inner, *weights)


def per_device(
    captured_waveform,
    element_lookup,
    combiner,
    pilot_syms,
    pilot_values,
    mod_order,
    conv_first,
    conv_rest,
    conv_bias,
    demap_in,
    demap_bias,
    demap_out,
):
    given, kept = beam_partials(captured_waveform, element_lookup, combiner)
    panels = lax.axis_size(PANEL)
    got = lax.ppermute(given, PANEL, [(p, p ^ 1) for p in range(panels)])
    pairs = (kept.astype(jnp.float32) + got.astype(jnp.float32)).astype(jnp.bfloat16)
    same_core = [list(range(core, panels, 2)) for core in range(2)]
    parts = lax.all_to_all(pairs, PANEL, 0, 0, axis_index_groups=same_core, tiled=True)
    own, *sent = sum_beams(parts, pilot_syms, pilot_values)
    both = (PANEL, SUB)
    count = lax.axis_size(both)
    pairs_of = [[(i, i + 1) for i in range(start, count - 1, 2)] for start in (0, 1)]
    got = [
        lax.ppermute(edge, both, pairs + [(j, i) for i, j in pairs]) for edge, pairs in zip(sent, pairs_of)
    ]
    c = combiner.shape[1]
    weights = (
        conv_first.reshape(-1, c),
        conv_rest.reshape(conv_rest.shape[0], -1, c),
        conv_bias,
        demap_in,
        demap_bias.reshape(1, -1),
        demap_out,
    )
    inner, patch = receive_interior(pilot_syms, mod_order, own, weights)
    return receive_edges(pilot_syms, mod_order, got, sent, patch, weights, inner)


def solution(mesh):
    in_specs = (
        P(None, None, SUB, PANEL),
        P(PANEL),
        P(PANEL, None),
        P(),
        P(None, (PANEL, SUB)),
        P((PANEL, SUB)),
        P(),
        P(),
        P(),
        P(),
        P(),
        P(),
    )
    out_specs = P(None, (PANEL, SUB), None)
    return jax.shard_map(
        per_device, mesh=mesh, in_specs=in_specs, out_specs=out_specs, check_vma=False
    )
```

```python
import jax
import jax.numpy as jnp
from jax import lax
from jax.experimental import pallas as pl
from jax.experimental.pallas import tpu as pltpu
from jax.sharding import PartitionSpec as P

RB_SC = 4
BITS = 8
PILOTS = 2
FIRST = 1
EDGE = 8
PANEL = "panel"
SUB = "sc"


def lookup_matrix(lookup, rows):
    n, c = rows.shape
    member = lax.broadcasted_iota(jnp.int32, (n, n), 0) == lookup % n
    picked = lax.dot_general(
        member.astype(jnp.bfloat16), rows, (((0,), (0,)), ((), ())), preferred_element_type=jnp.float32
    ).astype(jnp.bfloat16)
    doubled = (
        lax.broadcasted_iota(jnp.int32, (2 * n, n), 0) // 2 == lax.broadcasted_iota(jnp.int32, (2 * n, n), 1)
    )
    w = jnp.dot(doubled.astype(jnp.bfloat16), picked, preferred_element_type=jnp.float32)
    lane = lax.broadcasted_iota(jnp.int32, w.shape, 1)
    turned = pltpu.roll(w, c // 2, 1) * jnp.where(lane < c // 2, -1.0, 1.0)
    odd = lax.broadcasted_iota(jnp.int32, w.shape, 0) % 2 == 1
    return jnp.where(odd, turned, w).astype(jnp.bfloat16)


def matrix_kernel_body(wave_ref, out_ref, blocks_ref, sems, matrix, parity):
    count, syms, subs, c = out_ref.shape
    k = wave_ref.shape[3]

    def fetch(i):
        return pltpu.make_async_copy(wave_ref.at[2 * i + parity], blocks_ref.at[i], sems.at[i])

    for i in range(count):
        fetch(i).start()
    weights = matrix()
    for first, last in ((0, count // 4), (count // 4, count)):
        for i in range(first, last):
            fetch(i).wait()
        lines = blocks_ref[first:last].reshape((last - first) * syms * subs, k)
        out_ref[first:last] = (
            jnp.dot(lines, weights, preferred_element_type=jnp.float32)
            .astype(jnp.bfloat16)
            .reshape(last - first, syms, subs, c)
        )


def given_kernel(lookup_ref, rows_ref, wave_ref, out_ref, matrix_ref, blocks_ref, lookup_buf, rows_buf, sems):
    count = out_ref.shape[0]
    copies = [
        pltpu.make_async_copy(lookup_ref, lookup_buf, sems.at[count]),
        pltpu.make_async_copy(rows_ref, rows_buf, sems.at[count + 1]),
    ]
    for copy in copies:
        copy.start()

    def matrix():
        for copy in copies:
            copy.wait()
        matrix_ref[...] = lookup_matrix(lookup_buf[...], rows_buf[...])
        return matrix_ref[...]

    parity = 1 - lax.axis_index(PANEL) % 2
    matrix_kernel_body(wave_ref, out_ref, blocks_ref, sems, matrix, parity)


def kept_kernel(matrix_ref, wave_ref, out_ref, blocks_ref, sems):
    parity = lax.axis_index(PANEL) % 2
    matrix_kernel_body(wave_ref, out_ref, blocks_ref, sems, lambda: matrix_ref[...], parity)


def beam_partials(wave, lookup, rows):
    groups, syms, subs, k = wave.shape
    n, c = rows.shape
    half = groups // 2
    lookup, rows, wave = (
        pltpu.with_memory_space_constraint(array, pltpu.HBM) for array in (lookup.reshape(1, -1), rows, wave)
    )
    hbm = pl.BlockSpec(memory_space=pltpu.HBM)
    vmem = pl.BlockSpec(memory_space=pltpu.VMEM)
    params = pltpu.CompilerParams(vmem_limit_bytes=8 * 2**20)
    out = jax.ShapeDtypeStruct((half, syms, subs, c), jnp.bfloat16)
    blocks = pltpu.VMEM((half, syms, subs, k), jnp.bfloat16)
    given, matrix = pl.pallas_call(
        given_kernel,
        in_specs=[hbm] * 3,
        out_specs=[vmem] * 2,
        out_shape=[out, jax.ShapeDtypeStruct((k, c), jnp.bfloat16)],
        scratch_shapes=[
            blocks,
            pltpu.VMEM((1, n), jnp.int32),
            pltpu.VMEM((n, c), jnp.bfloat16),
            pltpu.SemaphoreType.DMA((half + 2,)),
        ],
        compiler_params=params,
        name="given",
    )(lookup, rows, wave)
    kept = pl.pallas_call(
        kept_kernel,
        in_specs=[vmem, hbm],
        out_specs=vmem,
        out_shape=out,
        scratch_shapes=[blocks, pltpu.SemaphoreType.DMA((half,))],
        compiler_params=params,
        cost_estimate=pl.CostEstimate(
            flops=2 * half * syms * subs * k * c, bytes_accessed=2 * half * syms * subs * k, transcendentals=0
        ),
        name="kept",
    )(matrix, wave)
    return given, kept


def as_column(row, count):
    diagonal = lax.broadcasted_iota(jnp.int32, (count, count), 0) == lax.broadcasted_iota(
        jnp.int32, (count, count), 1
    )
    return jnp.sum(jnp.where(diagonal, jnp.broadcast_to(row, (count, count)), 0.0), axis=1, keepdims=True)


def estimate_of(beams, pilot_re, pilot_im):
    c = beams.shape[-1]
    return beams * pilot_re + pltpu.roll(beams, c // 2, beams.ndim - 1) * pilot_im


def signed_pilots(pilot_ref, c):
    s = pilot_ref.shape[1]
    re = jnp.broadcast_to(as_column(pilot_ref[0:1, :], s), (s, c))
    im = jnp.broadcast_to(as_column(pilot_ref[1:2, :], s), (s, c))
    lane = lax.broadcasted_iota(jnp.int32, (s, c), 1)
    return re, jnp.where(lane < c // 2, im, -im)


def position():
    blocks = lax.axis_size(SUB)
    return lax.axis_index(PANEL) * blocks + lax.axis_index(SUB), lax.axis_size(PANEL) * blocks


def first_half(rows, low, high):
    return jnp.where(lax.broadcasted_iota(jnp.int32, rows, len(rows) - 2) < EDGE // 2, low, high)


def sum_kernel(syms_ref, order_ref, pilot_ref, parts_ref, *refs):
    *weights, own_ref, tail_ref, head_ref, llr_ref, patch_ref, wide_ref, even_ref, odd_ref, beams_ref = refs
    panels, syms, subs, c = parts_ref.shape
    for t in range(syms):
        total = parts_ref[0, t].astype(jnp.float32)
        for p in range(1, panels):
            total = total + parts_ref[p, t].astype(jnp.float32)
        beams_ref[t] = total.astype(jnp.bfloat16).astype(jnp.float32)
    re, im = signed_pilots(pilot_ref, c)
    for i in range(PILOTS):
        beams_ref[syms + i] = estimate_of(beams_ref[syms_ref[i]], re, im)
    half = EDGE // 2
    even = beams_ref[:, pl.ds(0, subs // 2, 2), :]
    odd = beams_ref[:, pl.ds(1, subs // 2, 2), :]
    own_ref[:, :, :c] = even.astype(jnp.bfloat16)
    own_ref[:, :, c:] = odd.astype(jnp.bfloat16)
    rows = (syms + PILOTS, EDGE, c)
    head = first_half(rows, even[:, :EDGE], pltpu.roll(odd[:, :EDGE], half, 1))
    tail = first_half(rows, pltpu.roll(even[:, subs // 2 - EDGE :], half, 1), odd[:, subs // 2 - EDGE :])
    tail_ref[...] = tail.astype(jnp.bfloat16)
    head_ref[...] = head.astype(jnp.bfloat16)

    @pl.when(waits_long())
    def _():
        interior(syms_ref, order_ref, own_ref, *weights, llr_ref, patch_ref, wide_ref, even_ref, odd_ref)


def late_kernel(syms_ref, order_ref, own_ref, *refs):
    *weights, early_llr_ref, early_patch_ref, llr_ref, patch_ref, wide_ref, even_ref, odd_ref = refs
    del early_llr_ref, early_patch_ref

    @pl.when(jnp.logical_not(waits_long()))
    def _():
        interior(syms_ref, order_ref, own_ref, *weights, llr_ref, patch_ref, wide_ref, even_ref, odd_ref)


def waits_long():
    return lax.axis_index(SUB) < FIRST


def interior_shapes(syms, subs, c, layers, bits):
    return [
        jax.ShapeDtypeStruct((syms, subs, bits), jnp.float32),
        jax.ShapeDtypeStruct((layers - 1, syms, EDGE, 2 * c), jnp.float32),
    ]


def interior_scratch(syms, subs, c):
    padded = (syms + 2) * (subs // 2)
    return [pltpu.VMEM((padded, lanes * c), jnp.bfloat16) for lanes in (8, 4, 4)]


def sum_beams(parts, pilot_syms, mod_order, pilot_values, weights):
    _, syms, subs, c = parts.shape
    smem = pl.BlockSpec(memory_space=pltpu.SMEM)
    vmem = pl.BlockSpec(memory_space=pltpu.VMEM)
    edge = jax.ShapeDtypeStruct((syms + PILOTS, EDGE, c), jnp.bfloat16)
    layers, bits = weights[1].shape[0] + 1, weights[-1].shape[1]
    return pl.pallas_call(
        sum_kernel,
        in_specs=[smem] * 2 + [vmem] * 8,
        out_specs=[vmem] * 5,
        out_shape=[
            jax.ShapeDtypeStruct((syms + PILOTS, subs // 2, 2 * c), jnp.bfloat16),
            edge,
            edge,
            *interior_shapes(syms, subs, c, layers, bits),
        ],
        scratch_shapes=[
            *interior_scratch(syms, subs, c),
            pltpu.VMEM((syms + PILOTS, subs, c), jnp.float32),
        ],
        compiler_params=pltpu.CompilerParams(vmem_limit_bytes=16 * 2**20),
        name="sum_beams",
    )(pilot_syms, mod_order, pilot_values, parts, *weights)


def pilot_rows(syms_ref, rows, syms):
    spread = []
    for t in range(syms):
        row = jnp.zeros(rows.shape[1:], rows.dtype)
        for i in range(PILOTS):
            row = jnp.where(syms_ref[i] == t, rows[i], row)
        spread.append(row)
    return jnp.stack(spread, 0)


def with_estimates(syms_ref, pairs, syms):
    c = pairs.shape[2] // 2
    beams, estimates = pairs[:syms], pilot_rows(syms_ref, pairs[syms:], syms)
    return jnp.concatenate([beams[..., :c], estimates[..., :c], beams[..., c:], estimates[..., c:]], axis=2)


def layer_sums(taps, kernel, bias):
    depth = kernel.shape[0] // 3
    zeros = jnp.zeros((depth // 3, kernel.shape[1]), kernel.dtype)
    total = jnp.concatenate([bias, bias], axis=1)
    for dt in range(3):
        part = kernel[dt * depth : (dt + 1) * depth]
        wide = jnp.concatenate(
            [jnp.concatenate([part, zeros], axis=0), jnp.concatenate([zeros, part], axis=0)], axis=1
        )
        total = total + jnp.dot(taps(dt), wide, preferred_element_type=jnp.float32)
    return jnp.maximum(total, 0.0)


def demapped(pairs, in_ref, in_bias_ref, out_w_ref):
    rows, c = pairs.shape[0], pairs.shape[1] // 2
    field = jnp.concatenate([pairs[:, :c], pairs[:, c:]], axis=0)
    hidden = jnp.dot(field, in_ref[...], preferred_element_type=jnp.float32)
    hidden = jnp.maximum(hidden + in_bias_ref[...], 0.0).astype(jnp.bfloat16)
    llr = jnp.dot(hidden, out_w_ref[...], preferred_element_type=jnp.float32)
    return llr[:rows], llr[rows:]


def bit_limits(order_ref, pairs, bits):
    row = lax.broadcasted_iota(jnp.int32, (len(pairs), bits), 0)
    limit = jnp.zeros((len(pairs), bits), jnp.int32)
    for block in sorted({2 * pair // RB_SC for pair in pairs}):
        at = [r for r, pair in enumerate(pairs) if 2 * pair // RB_SC == block]
        limit = jnp.where((row >= at[0]) & (row <= at[-1]), 2 * order_ref[block], limit)
    return limit


def store_llr(ref, llrs, limit, syms_ref):
    rows = limit.shape[0]
    bit = lax.broadcasted_iota(jnp.int32, limit.shape, 1) % BITS
    for t in range(ref.shape[0]):
        data = jnp.where((syms_ref[0] == t) | (syms_ref[1] == t), 0, 1)
        keep = bit < limit * data
        for side, llr in enumerate(llrs):
            ref[t, pl.ds(side, rows, 2), :] = jnp.where(keep, llr[t * rows : (t + 1) * rows], 0.0)


def interior(
    syms_ref, order_ref, own_ref, first_ref, rest_ref, bias_ref, in_ref, in_bias_ref, out_w_ref,
    llr_ref, patch_ref, wide_ref, even_ref, odd_ref,
):
    syms, pairs, c2 = own_ref.shape
    syms = syms - PILOTS
    layers = rest_ref.shape[0] + 1
    rows = syms * pairs
    for ref in (wide_ref, even_ref, odd_ref):
        ref[0:pairs] = jnp.zeros((pairs, ref.shape[1]), jnp.bfloat16)
        ref[pairs + rows :] = jnp.zeros((pairs, ref.shape[1]), jnp.bfloat16)

    def put(ref, whole):
        lanes = whole.shape[1]
        ref[pairs : pairs + rows, :lanes] = whole.astype(jnp.bfloat16)
        ref[pairs : pairs + rows, lanes:] = pltpu.roll(whole, rows - 1, 0).astype(jnp.bfloat16)

    field = with_estimates(syms_ref, own_ref[...].astype(jnp.float32), syms)
    put(wide_ref, field.reshape(rows, 2 * c2))
    src = wide_ref
    for layer in range(1, layers + 1):
        kernel = first_ref[...] if layer == 1 else rest_ref[layer - 2]
        total = layer_sums(
            lambda dt, src=src: src[dt * pairs : dt * pairs + rows], kernel, bias_ref[layer - 1 : layer, :]
        )
        if layer == layers:
            break
        src = (even_ref, odd_ref)[layer % 2]
        put(src, total)
        spread = total.reshape(syms, pairs, c2)
        last = pairs - 2 - layer
        group = last // 8 * 8
        low = pltpu.roll(spread[:, :8], 2, 1)
        high = spread[:, group : group + 8]
        if last % 8 != 4:
            high = pltpu.roll(high, (4 - last % 8) % 8, 1)
        patch_ref[layer - 1] = first_half((syms, 8, c2), low, high)
    final = pltpu.roll(total, layers // 2, 0).astype(jnp.bfloat16)
    llrs = demapped(final, in_ref, in_bias_ref, out_w_ref)
    store_llr(llr_ref, llrs, bit_limits(order_ref, list(range(pairs)), llr_ref.shape[2]), syms_ref)


def edge_kernel(
    syms_ref, order_ref, left_ref, right_ref, tail_ref, head_ref, patch_ref, inner_ref,
    first_ref, rest_ref, bias_ref, in_ref, in_bias_ref, out_w_ref,
    llr_ref, llr_buf, sems,
):
    syms, half = left_ref.shape[0] - PILOTS, EDGE // 2
    layers = rest_ref.shape[0] + 1
    subs = llr_ref.shape[1]
    c2 = 2 * left_ref.shape[2]
    rows = syms * EDGE
    middle = pl.ds(EDGE, subs - 2 * EDGE)
    inner_copy = pltpu.make_async_copy(inner_ref.at[:, middle], llr_ref.at[:, middle], sems.at[2])
    inner_copy.start()

    def paired(ref):
        columns = ref[...].astype(jnp.float32)
        return jnp.concatenate([columns, pltpu.roll(columns, half, 1)], axis=2)

    def row_of(shape):
        return lax.broadcasted_iota(jnp.int32, shape, len(shape) - 2)

    def convolved(this, after, kernel, bias):
        both = jnp.concatenate([this, after], axis=2)
        lanes = both.shape[2]
        padding = jnp.zeros((1, EDGE, lanes), jnp.float32)
        padded = jnp.concatenate([padding, both, padding], axis=0)
        return layer_sums(
            lambda dt: padded[dt : dt + syms].reshape(rows, lanes).astype(jnp.bfloat16), kernel, bias
        ).reshape(syms, EDGE, c2)

    at, blocks = position()
    left, right, tail, head = (paired(ref) for ref in (left_ref, right_ref, tail_ref, head_ref))
    low = first_half(left.shape, left, pltpu.roll(head, half, 1))
    high = first_half(left.shape, tail, pltpu.roll(right, half, 1))
    this = first_half(low.shape, pltpu.roll(low, EDGE - 1, 1), pltpu.roll(high, 2, 1))
    after = first_half(low.shape, pltpu.roll(low, EDGE - 2, 1), pltpu.roll(high, 1, 1))
    total = convolved(
        with_estimates(syms_ref, this, syms), with_estimates(syms_ref, after, syms),
        first_ref[...], bias_ref[0:1, :],
    )
    row = row_of((EDGE, c2))
    odd = lax.broadcasted_iota(jnp.int32, (EDGE, c2), 1) // (c2 // 2)
    for layer in range(1, layers):
        below = (row < half) & (2 * row + odd < layers - layer) & (at == 0)
        above = (row >= half) & (2 * (row - half) + odd >= 2 + layer) & (at == blocks - 1)
        total = jnp.where((below | above)[None], 0.0, total)
        patch = patch_ref[layer - 1]
        rows_of = row_of(total.shape)
        this = jnp.where(rows_of < half, total, jnp.where(rows_of == half, patch, pltpu.roll(total, 1, 1)))
        after = jnp.where(
            rows_of < half - 1, pltpu.roll(total, EDGE - 1, 1), jnp.where(rows_of == half - 1, patch, total)
        )
        total = convolved(this, after, rest_ref[layer - 1], bias_ref[layer : layer + 1, :])
    llrs = demapped(total.reshape(rows, c2).astype(jnp.bfloat16), in_ref, in_bias_ref, out_w_ref)
    columns = [*range(half), *range(subs // 2 - half, subs // 2)]
    store_llr(llr_buf, llrs, bit_limits(order_ref, columns, llr_ref.shape[2]), syms_ref)
    copies = [
        pltpu.make_async_copy(
            llr_buf.at[:, pl.ds(side * EDGE, EDGE)], llr_ref.at[:, pl.ds(start, EDGE)], sems.at[side]
        )
        for side, start in enumerate((0, subs - EDGE))
    ]
    for copy in copies:
        copy.start()
    inner_copy.wait()
    for copy in copies:
        copy.wait()


def receive_interior(pilot_syms, mod_order, own, weights, early):
    syms, pairs, c2 = own.shape
    syms = syms - PILOTS
    layers, bits = weights[1].shape[0] + 1, weights[-1].shape[1]
    smem = pl.BlockSpec(memory_space=pltpu.SMEM)
    vmem = pl.BlockSpec(memory_space=pltpu.VMEM)
    return pl.pallas_call(
        late_kernel,
        in_specs=[smem] * 2 + [vmem] * 9,
        out_specs=[vmem] * 2,
        out_shape=interior_shapes(syms, 2 * pairs, c2 // 2, layers, bits),
        input_output_aliases={9: 0, 10: 1},
        scratch_shapes=interior_scratch(syms, 2 * pairs, c2 // 2),
        compiler_params=pltpu.CompilerParams(vmem_limit_bytes=16 * 2**20),
        cost_estimate=pl.CostEstimate(flops=10**9, bytes_accessed=4 * 10**6, transcendentals=0),
        name="interior",
    )(pilot_syms, mod_order, own, *weights, *early)


def receive_edges(pilot_syms, mod_order, got, sent, patch, weights, inner):
    syms, subs, bits = inner.shape
    smem = pl.BlockSpec(memory_space=pltpu.SMEM)
    vmem = pl.BlockSpec(memory_space=pltpu.VMEM)
    return pl.pallas_call(
        edge_kernel,
        in_specs=[smem] * 2 + [vmem] * 12,
        out_specs=pl.BlockSpec(memory_space=pltpu.HBM),
        out_shape=pltpu.HBM(inner.shape, jnp.float32),
        scratch_shapes=[
            pltpu.VMEM((syms, 2 * EDGE, bits), jnp.float32),
            pltpu.SemaphoreType.DMA((3,)),
        ],
        compiler_params=pltpu.CompilerParams(vmem_limit_bytes=16 * 2**20),
        cost_estimate=pl.CostEstimate(flops=5 * 10**8, bytes_accessed=4 * 10**6, transcendentals=0),
        name="edges",
    )(pilot_syms, mod_order, *got, *sent, patch, inner, *weights)


def per_device(
    captured_waveform,
    element_lookup,
    combiner,
    pilot_syms,
    pilot_values,
    mod_order,
    conv_first,
    conv_rest,
    conv_bias,
    demap_in,
    demap_bias,
    demap_out,
):
    given, kept = beam_partials(captured_waveform, element_lookup, combiner)
    panels = lax.axis_size(PANEL)
    got = lax.ppermute(given, PANEL, [(p, p ^ 1) for p in range(panels)])
    pairs = (kept.astype(jnp.float32) + got.astype(jnp.float32)).astype(jnp.bfloat16)
    same_core = [list(range(core, panels, 2)) for core in range(2)]
    parts = lax.all_to_all(pairs, PANEL, 0, 0, axis_index_groups=same_core, tiled=True)
    c = combiner.shape[1]
    weights = (
        conv_first.reshape(-1, c),
        conv_rest.reshape(conv_rest.shape[0], -1, c),
        conv_bias,
        demap_in,
        demap_bias.reshape(1, -1),
        demap_out,
    )
    own, tail, head, *early = sum_beams(parts, pilot_syms, mod_order, pilot_values, weights)
    both = (PANEL, SUB)
    count = lax.axis_size(both)
    left = lax.ppermute(tail, both, [(i, i + 1) for i in range(count - 1)])
    right = lax.ppermute(head, both, [(i + 1, i) for i in range(count - 1)])
    inner, patch = receive_interior(pilot_syms, mod_order, own, weights, early)
    return receive_edges(pilot_syms, mod_order, (left, right), (tail, head), patch, weights, inner)


def solution(mesh):
    in_specs = (
        P(None, None, SUB, PANEL),
        P(PANEL),
        P(PANEL, None),
        P(),
        P(None, (PANEL, SUB)),
        P((PANEL, SUB)),
        P(),
        P(),
        P(),
        P(),
        P(),
        P(),
    )
    out_specs = P(None, (PANEL, SUB), None)
    return jax.shard_map(
        per_device, mesh=mesh, in_specs=in_specs, out_specs=out_specs, check_vma=False
    )
```

```python
import jax
import jax.numpy as jnp
from jax import lax
from jax.experimental import pallas as pl
from jax.experimental.pallas import tpu as pltpu
from jax.sharding import PartitionSpec as P

RB_SC = 4
BITS = 8
PILOTS = 2
FIRST = 1
EDGE = 8
PANEL = "panel"
SUB = "sc"


def lookup_matrix(lookup, rows):
    n, c = rows.shape
    member = lax.broadcasted_iota(jnp.int32, (n, n), 0) == lookup % n
    picked = lax.dot_general(
        member.astype(jnp.bfloat16), rows, (((0,), (0,)), ((), ())), preferred_element_type=jnp.float32
    ).astype(jnp.bfloat16)
    doubled = (
        lax.broadcasted_iota(jnp.int32, (2 * n, n), 0) // 2 == lax.broadcasted_iota(jnp.int32, (2 * n, n), 1)
    )
    w = jnp.dot(doubled.astype(jnp.bfloat16), picked, preferred_element_type=jnp.float32)
    lane = lax.broadcasted_iota(jnp.int32, w.shape, 1)
    turned = pltpu.roll(w, c // 2, 1) * jnp.where(lane < c // 2, -1.0, 1.0)
    odd = lax.broadcasted_iota(jnp.int32, w.shape, 0) % 2 == 1
    return jnp.where(odd, turned, w).astype(jnp.bfloat16)


def matrix_kernel_body(wave_ref, out_ref, blocks_ref, sems, matrix, parity):
    count, syms, subs, c = out_ref.shape
    k = wave_ref.shape[3]

    def fetch(i):
        return pltpu.make_async_copy(wave_ref.at[2 * i + parity], blocks_ref.at[i], sems.at[i])

    for i in range(count):
        fetch(i).start()
    weights = matrix()
    for first, last in ((0, count // 4), (count // 4, count)):
        for i in range(first, last):
            fetch(i).wait()
        lines = blocks_ref[first:last].reshape((last - first) * syms * subs, k)
        out_ref[first:last] = (
            jnp.dot(lines, weights, preferred_element_type=jnp.float32)
            .astype(jnp.bfloat16)
            .reshape(last - first, syms, subs, c)
        )


def given_kernel(lookup_ref, rows_ref, wave_ref, out_ref, matrix_ref, blocks_ref, lookup_buf, rows_buf, sems):
    count = out_ref.shape[0]
    copies = [
        pltpu.make_async_copy(lookup_ref, lookup_buf, sems.at[count]),
        pltpu.make_async_copy(rows_ref, rows_buf, sems.at[count + 1]),
    ]
    for copy in copies:
        copy.start()

    def matrix():
        for copy in copies:
            copy.wait()
        matrix_ref[...] = lookup_matrix(lookup_buf[...], rows_buf[...])
        return matrix_ref[...]

    parity = 1 - lax.axis_index(PANEL) % 2
    matrix_kernel_body(wave_ref, out_ref, blocks_ref, sems, matrix, parity)


def kept_kernel(
    matrix_ref, syms_ref, order_ref, pilot_ref, wave_ref, out_ref, chosen_ref, keep_ref, pilots_ref, blocks_ref, sems
):
    parity = lax.axis_index(PANEL) % 2
    matrix_kernel_body(wave_ref, out_ref, blocks_ref, sems, lambda: matrix_ref[...], parity)
    for i in range(PILOTS):
        at = jnp.broadcast_to(entry(syms_ref[...].astype(jnp.float32), i), chosen_ref.shape[1:])
        row = lax.broadcasted_iota(jnp.int32, chosen_ref.shape[1:], 0)
        chosen_ref[i] = jnp.where(row.astype(jnp.float32) == at, 1.0, 0.0)
    subs, bits = keep_ref.shape
    blocks = order_ref.shape[1]
    mine = lax.broadcasted_iota(jnp.int32, (subs, blocks), 0) // RB_SC == lax.broadcasted_iota(
        jnp.int32, (subs, blocks), 1
    )
    orders = jnp.broadcast_to(order_ref[...].astype(jnp.float32), (subs, blocks))
    limit = 2.0 * jnp.sum(jnp.where(mine, orders, 0.0), axis=1, keepdims=True)
    bit = lax.broadcasted_iota(jnp.int32, (subs, bits), 1) % BITS
    keep_ref[...] = jnp.where(bit.astype(jnp.float32) < limit, 1.0, 0.0)
    pilots_ref[0], pilots_ref[1] = signed_pilots(pilot_ref, pilots_ref.shape[2])


def beam_partials(wave, lookup, rows, pilot_syms, mod_order, pilot_values, bits):
    groups, syms, subs, k = wave.shape
    n, c = rows.shape
    half = groups // 2
    lookup, rows, wave = (
        pltpu.with_memory_space_constraint(array, pltpu.HBM) for array in (lookup.reshape(1, -1), rows, wave)
    )
    hbm = pl.BlockSpec(memory_space=pltpu.HBM)
    vmem = pl.BlockSpec(memory_space=pltpu.VMEM)
    params = pltpu.CompilerParams(vmem_limit_bytes=8 * 2**20)
    out = jax.ShapeDtypeStruct((half, syms, subs, c), jnp.bfloat16)
    blocks = pltpu.VMEM((half, syms, subs, k), jnp.bfloat16)
    given, matrix = pl.pallas_call(
        given_kernel,
        in_specs=[hbm] * 3,
        out_specs=[vmem] * 2,
        out_shape=[out, jax.ShapeDtypeStruct((k, c), jnp.bfloat16)],
        scratch_shapes=[
            blocks,
            pltpu.VMEM((1, n), jnp.int32),
            pltpu.VMEM((n, c), jnp.bfloat16),
            pltpu.SemaphoreType.DMA((half + 2,)),
        ],
        compiler_params=params,
        name="given",
    )(lookup, rows, wave)
    kept, *facts = pl.pallas_call(
        kept_kernel,
        in_specs=[vmem] * 4 + [hbm],
        out_specs=[vmem] * 4,
        out_shape=[
            out,
            jax.ShapeDtypeStruct((PILOTS, pl.cdiv(syms, 8) * 8, c), jnp.float32),
            jax.ShapeDtypeStruct((subs, bits), jnp.float32),
            jax.ShapeDtypeStruct((2, subs, c), jnp.float32),
        ],
        scratch_shapes=[blocks, pltpu.SemaphoreType.DMA((half,))],
        compiler_params=params,
        cost_estimate=pl.CostEstimate(
            flops=2 * half * syms * subs * k * c, bytes_accessed=2 * half * syms * subs * k, transcendentals=0
        ),
        name="kept",
    )(matrix, pilot_syms.reshape(1, -1), mod_order.reshape(1, -1), pilot_values, wave)
    return given, kept, facts


def entry(row, i):
    lane = lax.broadcasted_iota(jnp.int32, row.shape, 1)
    return jnp.sum(jnp.where(lane == i, row, 0.0), axis=1, keepdims=True)


def chosen_rows(chosen_ref, i, t, like):
    return jnp.broadcast_to(chosen_ref[i, t : t + 1, :], like.shape[-2:]) > 0.0


def as_column(row, count):
    diagonal = lax.broadcasted_iota(jnp.int32, (count, count), 0) == lax.broadcasted_iota(
        jnp.int32, (count, count), 1
    )
    return jnp.sum(jnp.where(diagonal, jnp.broadcast_to(row, (count, count)), 0.0), axis=1, keepdims=True)


def estimate_of(beams, pilot_re, pilot_im):
    c = beams.shape[-1]
    return beams * pilot_re + pltpu.roll(beams, c // 2, beams.ndim - 1) * pilot_im


def signed_pilots(pilot_ref, c):
    s = pilot_ref.shape[1]
    re = jnp.broadcast_to(as_column(pilot_ref[0:1, :], s), (s, c))
    im = jnp.broadcast_to(as_column(pilot_ref[1:2, :], s), (s, c))
    lane = lax.broadcasted_iota(jnp.int32, (s, c), 1)
    return re, jnp.where(lane < c // 2, im, -im)


def position():
    blocks = lax.axis_size(SUB)
    return lax.axis_index(PANEL) * blocks + lax.axis_index(SUB), lax.axis_size(PANEL) * blocks


def sum_kernel(chosen_ref, keep_ref, pilots_ref, parts_ref, *refs):
    *weights, own_ref, tail_ref, head_ref, llr_ref, patch_ref, wide_ref, even_ref, odd_ref = refs
    panels, syms, subs, c = parts_ref.shape

    def put(t, values):
        own_ref[t] = values
        head_ref[t] = values[:EDGE]
        tail_ref[t] = values[subs - EDGE :]

    at_pilots = [jnp.zeros((subs, c), jnp.float32) for _ in range(PILOTS)]
    for t in range(syms):
        total = parts_ref[0, t].astype(jnp.float32)
        for p in range(1, panels):
            total = total + parts_ref[p, t].astype(jnp.float32)
        beams = total.astype(jnp.bfloat16)
        put(t, beams)
        for i in range(PILOTS):
            at_pilots[i] = jnp.where(chosen_rows(chosen_ref, i, t, beams), beams.astype(jnp.float32), at_pilots[i])
    for i in range(PILOTS):
        put(syms + i, estimate_of(at_pilots[i], pilots_ref[0], pilots_ref[1]).astype(jnp.bfloat16))

    @pl.when(waits_long())
    def _():
        interior(chosen_ref, keep_ref, own_ref, *weights, llr_ref, patch_ref, wide_ref, even_ref, odd_ref)


def late_kernel(chosen_ref, keep_ref, own_ref, *refs):
    *weights, early_llr_ref, early_patch_ref, llr_ref, patch_ref, wide_ref, even_ref, odd_ref = refs
    del early_llr_ref, early_patch_ref

    @pl.when(jnp.logical_not(waits_long()))
    def _():
        interior(chosen_ref, keep_ref, own_ref, *weights, llr_ref, patch_ref, wide_ref, even_ref, odd_ref)


def waits_long():
    return lax.axis_index(SUB) < FIRST


def interior_shapes(syms, subs, c, layers, bits):
    return [
        jax.ShapeDtypeStruct((syms, subs, bits), jnp.float32),
        jax.ShapeDtypeStruct((layers - 1, syms, 2 * EDGE, c), jnp.float32),
    ]


def interior_scratch(syms, subs, c):
    padded = (syms + 2) * subs
    return [pltpu.VMEM((padded, lanes * c), jnp.bfloat16) for lanes in (2, 1, 1)]


def sum_beams(parts, facts, weights):
    _, syms, subs, c = parts.shape
    vmem = pl.BlockSpec(memory_space=pltpu.VMEM)
    edge = jax.ShapeDtypeStruct((syms + PILOTS, EDGE, c), jnp.bfloat16)
    layers, bits = weights[1].shape[0] + 1, weights[-1].shape[1]
    return pl.pallas_call(
        sum_kernel,
        in_specs=[vmem] * 10,
        out_specs=[vmem] * 5,
        out_shape=[
            jax.ShapeDtypeStruct((syms + PILOTS, subs, c), jnp.bfloat16),
            edge,
            edge,
            *interior_shapes(syms, subs, c, layers, bits),
        ],
        scratch_shapes=interior_scratch(syms, subs, c),
        compiler_params=pltpu.CompilerParams(vmem_limit_bytes=16 * 2**20),
        name="sum_beams",
    )(*facts, parts, *weights)


def pilot_rows(chosen_ref, rows, syms):
    spread = []
    for t in range(syms):
        row = jnp.zeros(rows.shape[1:], rows.dtype)
        for i in range(PILOTS):
            row = jnp.where(chosen_rows(chosen_ref, i, t, row), rows[i], row)
        spread.append(row)
    return jnp.stack(spread, 0)


def with_estimates(chosen_ref, pieces, syms):
    return jnp.concatenate([pieces[:syms], pilot_rows(chosen_ref, pieces[syms:], syms)], axis=2)


def taps_of(kernel, dt, dc):
    depth = kernel.shape[0] // 9
    return kernel[(3 * dt + dc) * depth : (3 * dt + dc + 1) * depth]


def demapped(field, in_ref, in_bias_ref, out_w_ref):
    hidden = jnp.dot(field, in_ref[...], preferred_element_type=jnp.float32)
    hidden = jnp.maximum(hidden + in_bias_ref[...], 0.0).astype(jnp.bfloat16)
    return jnp.dot(hidden, out_w_ref[...], preferred_element_type=jnp.float32)


def store_llr(ref, llr, keep, chosen_ref):
    rows = keep.shape[0]
    for t in range(ref.shape[0]):
        kept = keep > 0.0
        for i in range(PILOTS):
            kept = kept & jnp.logical_not(chosen_rows(chosen_ref, i, t, keep))
        ref[t] = jnp.where(kept, llr[t * rows : (t + 1) * rows], 0.0)


def interior(
    chosen_ref, keep_ref, own_ref, first_ref, rest_ref, bias_ref, in_ref, in_bias_ref, out_w_ref,
    llr_ref, patch_ref, wide_ref, even_ref, odd_ref,
):
    syms, subs, c = own_ref.shape
    syms = syms - PILOTS
    layers = rest_ref.shape[0] + 1
    rows = syms * subs
    for ref in (wide_ref, even_ref, odd_ref):
        ref[0:subs] = jnp.zeros((subs, ref.shape[1]), jnp.bfloat16)
        ref[subs + rows :] = jnp.zeros((subs, ref.shape[1]), jnp.bfloat16)
    wide_ref[subs : subs + rows, :c] = own_ref[:syms].reshape(rows, c)
    estimates = pilot_rows(chosen_ref, own_ref[syms:].astype(jnp.float32), syms)
    for t in range(syms):
        wide_ref[subs * (t + 1) : subs * (t + 2), c:] = estimates[t].astype(jnp.bfloat16)
    src = wide_ref
    for layer in range(1, layers + 1):
        kernel = first_ref[...] if layer == 1 else rest_ref[layer - 2]
        taps = jnp.concatenate([src[dt * subs : dt * subs + rows] for dt in range(3)], axis=1)
        wide = jnp.concatenate(
            [jnp.concatenate([taps_of(kernel, dt, dc) for dc in range(3)], axis=1) for dt in range(3)], axis=0
        )
        sums = jnp.dot(taps, wide, preferred_element_type=jnp.float32)
        total = sums[:, :c] + bias_ref[layer - 1 : layer, :]
        for dc in range(1, 3):
            total = total + pltpu.roll(sums[:, dc * c : (dc + 1) * c], rows - dc, 0)
        total = jnp.maximum(total, 0.0)
        if layer == layers:
            break
        src = (even_ref, odd_ref)[layer % 2]
        src[subs : subs + rows] = total.astype(jnp.bfloat16)
        spread = total.reshape(syms, subs, c)
        last = subs - 4 - 2 * layer
        group, place = last // EDGE * EDGE, last % EDGE
        high = spread[:, group : group + EDGE]
        if place != EDGE - 2:
            high = pltpu.roll(high, EDGE - 2 - place, 1)
        patch_ref[layer - 1] = jnp.concatenate([pltpu.roll(spread[:, :EDGE], EDGE - 2, 1), high], axis=1)
    final = pltpu.roll(total, layers, 0).astype(jnp.bfloat16)
    llr = demapped(final, in_ref, in_bias_ref, out_w_ref)
    store_llr(llr_ref, llr, keep_ref[...], chosen_ref)


def edge_kernel(
    chosen_ref, keep_ref, left_ref, right_ref, tail_ref, head_ref, patch_ref, inner_ref,
    first_ref, rest_ref, bias_ref, in_ref, in_bias_ref, out_w_ref,
    llr_ref, llr_buf, sems,
):
    syms, c = left_ref.shape[0] - PILOTS, left_ref.shape[2]
    layers = rest_ref.shape[0] + 1
    subs = llr_ref.shape[1]
    width = 2 * EDGE
    rows = syms * width
    middle = pl.ds(EDGE, subs - 2 * EDGE)
    inner_copy = pltpu.make_async_copy(inner_ref.at[:, middle], llr_ref.at[:, middle], sems.at[2])
    inner_copy.start()

    def joined(before, after, start):
        if start == 0:
            return before
        if start == EDGE:
            return after
        row = lax.broadcasted_iota(jnp.int32, before.shape, 1)
        turn = EDGE - start
        return jnp.where(row < turn, pltpu.roll(before, turn, 1), pltpu.roll(after, turn, 1))

    def convolved(shifted, kernel, bias):
        field = jnp.concatenate(shifted, axis=2)
        wide = jnp.concatenate(
            [jnp.concatenate([taps_of(kernel, dt, dc) for dt in range(3)], axis=1) for dc in range(3)], axis=0
        )
        sums = jnp.dot(
            field.reshape(rows, field.shape[2]).astype(jnp.bfloat16), wide, preferred_element_type=jnp.float32
        ).reshape(syms, width, 3 * c)
        nothing = jnp.zeros((1, width, c), jnp.float32)
        total = sums[:, :, c : 2 * c] + bias[None]
        total = total + jnp.concatenate([nothing, sums[:-1, :, :c]], axis=0)
        total = total + jnp.concatenate([sums[1:, :, 2 * c :], nothing], axis=0)
        return jnp.maximum(total, 0.0)

    at, blocks = position()
    left, right, tail, head = (ref[...].astype(jnp.float32) for ref in (left_ref, right_ref, tail_ref, head_ref))
    shifted = []
    for dc in range(3):
        low = joined(left, head, EDGE - layers + dc)
        high = joined(tail, right, EDGE - 4 + dc)
        shifted.append(with_estimates(chosen_ref, jnp.concatenate([low, high], axis=1), syms))
    total = convolved(shifted, first_ref[...], bias_ref[0:1, :])
    row = lax.broadcasted_iota(jnp.int32, (width, c), 0)
    for layer in range(1, layers):
        below = (row < layers - layer) & (at == 0)
        above = (row >= EDGE + 2 + layer) & (at == blocks - 1)
        total = jnp.where((below | above)[None], 0.0, total)
        patch = patch_ref[layer - 1]
        inner_low, inner_high = patch[:, :EDGE], patch[:, EDGE:]
        low, high = total[:, :EDGE], total[:, EDGE:]
        shifted = [
            jnp.concatenate([joined(low, inner_low, dc), joined(inner_high, high, EDGE - 2 + dc)], axis=1)
            for dc in range(3)
        ]
        total = convolved(shifted, rest_ref[layer - 1], bias_ref[layer : layer + 1, :])
    llr = demapped(total.reshape(rows, c).astype(jnp.bfloat16), in_ref, in_bias_ref, out_w_ref)
    keep = jnp.concatenate([keep_ref[:EDGE], keep_ref[subs - EDGE :]], axis=0)
    store_llr(llr_buf, llr, keep, chosen_ref)
    copies = [
        pltpu.make_async_copy(
            llr_buf.at[:, pl.ds(side * EDGE, EDGE)], llr_ref.at[:, pl.ds(start, EDGE)], sems.at[side]
        )
        for side, start in enumerate((0, subs - EDGE))
    ]
    for copy in copies:
        copy.start()
    inner_copy.wait()
    for copy in copies:
        copy.wait()


def receive_interior(facts, own, weights, early):
    syms, subs, c = own.shape
    syms = syms - PILOTS
    layers, bits = weights[1].shape[0] + 1, weights[-1].shape[1]
    vmem = pl.BlockSpec(memory_space=pltpu.VMEM)
    return pl.pallas_call(
        late_kernel,
        in_specs=[vmem] * 11,
        out_specs=[vmem] * 2,
        out_shape=interior_shapes(syms, subs, c, layers, bits),
        input_output_aliases={9: 0, 10: 1},
        scratch_shapes=interior_scratch(syms, subs, c),
        compiler_params=pltpu.CompilerParams(vmem_limit_bytes=16 * 2**20),
        cost_estimate=pl.CostEstimate(flops=10**9, bytes_accessed=4 * 10**6, transcendentals=0),
        name="interior",
    )(*facts[:2], own, *weights, *early)


def receive_edges(facts, got, sent, patch, weights, inner):
    syms, subs, bits = inner.shape
    vmem = pl.BlockSpec(memory_space=pltpu.VMEM)
    return pl.pallas_call(
        edge_kernel,
        in_specs=[vmem] * 14,
        out_specs=pl.BlockSpec(memory_space=pltpu.HBM),
        out_shape=pltpu.HBM(inner.shape, jnp.float32),
        scratch_shapes=[
            pltpu.VMEM((syms, 2 * EDGE, bits), jnp.float32),
            pltpu.SemaphoreType.DMA((3,)),
        ],
        compiler_params=pltpu.CompilerParams(vmem_limit_bytes=16 * 2**20),
        cost_estimate=pl.CostEstimate(flops=5 * 10**8, bytes_accessed=4 * 10**6, transcendentals=0),
        name="edges",
    )(*facts[:2], *got, *sent, patch, inner, *weights)


def per_device(
    captured_waveform,
    element_lookup,
    combiner,
    pilot_syms,
    pilot_values,
    mod_order,
    conv_first,
    conv_rest,
    conv_bias,
    demap_in,
    demap_bias,
    demap_out,
):
    given, kept, facts = beam_partials(
        captured_waveform, element_lookup, combiner, pilot_syms, mod_order, pilot_values, demap_out.shape[1]
    )
    panels = lax.axis_size(PANEL)
    got = lax.ppermute(given, PANEL, [(p, p ^ 1) for p in range(panels)])
    pairs = (kept.astype(jnp.float32) + got.astype(jnp.float32)).astype(jnp.bfloat16)
    same_core = [list(range(core, panels, 2)) for core in range(2)]
    parts = lax.all_to_all(pairs, PANEL, 0, 0, axis_index_groups=same_core, tiled=True)
    c = combiner.shape[1]
    weights = (
        conv_first.reshape(-1, c),
        conv_rest.reshape(conv_rest.shape[0], -1, c),
        conv_bias,
        demap_in,
        demap_bias.reshape(1, -1),
        demap_out,
    )
    own, tail, head, *early = sum_beams(parts, facts, weights)
    both = (PANEL, SUB)
    count = lax.axis_size(both)
    left = lax.ppermute(tail, both, [(i, i + 1) for i in range(count - 1)])
    right = lax.ppermute(head, both, [(i + 1, i) for i in range(count - 1)])
    inner, patch = receive_interior(facts, own, weights, early)
    return receive_edges(facts, (left, right), (tail, head), patch, weights, inner)


def solution(mesh):
    in_specs = (
        P(None, None, SUB, PANEL),
        P(PANEL),
        P(PANEL, None),
        P(),
        P(None, (PANEL, SUB)),
        P((PANEL, SUB)),
        P(),
        P(),
        P(),
        P(),
        P(),
        P(),
    )
    out_specs = P(None, (PANEL, SUB), None)
    return jax.shard_map(
        per_device, mesh=mesh, in_specs=in_specs, out_specs=out_specs, check_vma=False
    )
```

```python
import jax
import jax.numpy as jnp
from jax import lax
from jax.experimental import pallas as pl
from jax.experimental.pallas import tpu as pltpu
from jax.sharding import PartitionSpec as P

RB_SC = 4
BITS = 8
PILOTS = 2
COPIES = 4
FIRST = 1
EDGE = 8
PANEL = "panel"
SUB = "sc"


def lookup_matrix(lookup, rows):
    n, c = rows.shape
    member = lax.broadcasted_iota(jnp.int32, (n, n), 0) == lookup % n
    picked = lax.dot_general(
        member.astype(jnp.bfloat16), rows, (((0,), (0,)), ((), ())), preferred_element_type=jnp.float32
    ).astype(jnp.bfloat16)
    doubled = (
        lax.broadcasted_iota(jnp.int32, (2 * n, n), 0) // 2 == lax.broadcasted_iota(jnp.int32, (2 * n, n), 1)
    )
    w = jnp.dot(doubled.astype(jnp.bfloat16), picked, preferred_element_type=jnp.float32)
    lane = lax.broadcasted_iota(jnp.int32, w.shape, 1)
    turned = pltpu.roll(w, c // 2, 1) * jnp.where(lane < c // 2, -1.0, 1.0)
    odd = lax.broadcasted_iota(jnp.int32, w.shape, 0) % 2 == 1
    return jnp.where(odd, turned, w).astype(jnp.bfloat16)


def matrix_kernel_body(wave_ref, out_ref, blocks_ref, sems, matrix, parity):
    count, syms, subs, c = out_ref.shape
    k = wave_ref.shape[4]
    step = count // COPIES

    def fetch(i):
        some = pl.ds(i * step, step)
        return pltpu.make_async_copy(wave_ref.at[some, parity], blocks_ref.at[some], sems.at[i])

    for i in range(COPIES):
        fetch(i).start()
    weights = matrix()
    for first, last in ((0, step), (step, count)):
        for i in range(first // step, last // step):
            fetch(i).wait()
        lines = blocks_ref[first:last].reshape((last - first) * syms * subs, k)
        out_ref[first:last] = (
            jnp.dot(lines, weights, preferred_element_type=jnp.float32)
            .astype(jnp.bfloat16)
            .reshape(last - first, syms, subs, c)
        )


def given_kernel(lookup_ref, rows_ref, wave_ref, out_ref, matrix_ref, blocks_ref, lookup_buf, rows_buf, sems):
    copies = [
        pltpu.make_async_copy(lookup_ref, lookup_buf, sems.at[COPIES]),
        pltpu.make_async_copy(rows_ref, rows_buf, sems.at[COPIES + 1]),
    ]
    for copy in copies:
        copy.start()

    def matrix():
        for copy in copies:
            copy.wait()
        matrix_ref[...] = lookup_matrix(lookup_buf[...], rows_buf[...])
        return matrix_ref[...]

    parity = 1 - lax.axis_index(PANEL) % 2
    matrix_kernel_body(wave_ref, out_ref, blocks_ref, sems, matrix, parity)


def kept_kernel(
    matrix_ref, syms_ref, order_ref, pilot_ref, wave_ref, out_ref, chosen_ref, keep_ref, pilots_ref, blocks_ref, sems
):
    def matrix():
        for i in range(PILOTS):
            at = jnp.broadcast_to(entry(syms_ref[...].astype(jnp.float32), i), chosen_ref.shape[1:])
            row = lax.broadcasted_iota(jnp.int32, chosen_ref.shape[1:], 0)
            chosen_ref[i] = jnp.where(row.astype(jnp.float32) == at, 1.0, 0.0)
        subs, bits = keep_ref.shape
        blocks = order_ref.shape[1]
        mine = lax.broadcasted_iota(jnp.int32, (subs, blocks), 0) // RB_SC == lax.broadcasted_iota(
            jnp.int32, (subs, blocks), 1
        )
        orders = jnp.broadcast_to(order_ref[...].astype(jnp.float32), (subs, blocks))
        limit = 2.0 * jnp.sum(jnp.where(mine, orders, 0.0), axis=1, keepdims=True)
        bit = lax.broadcasted_iota(jnp.int32, (subs, bits), 1) % BITS
        keep_ref[...] = jnp.where(bit.astype(jnp.float32) < limit, 1.0, 0.0)
        pilots_ref[0], pilots_ref[1] = signed_pilots(pilot_ref, pilots_ref.shape[2])
        return matrix_ref[...]

    parity = lax.axis_index(PANEL) % 2
    matrix_kernel_body(wave_ref, out_ref, blocks_ref, sems, matrix, parity)


def beam_partials(wave, lookup, rows, pilot_syms, mod_order, pilot_values, bits):
    groups, syms, subs, k = wave.shape
    n, c = rows.shape
    half = groups // 2
    lookup, rows, wave = (
        pltpu.with_memory_space_constraint(array, pltpu.HBM)
        for array in (lookup.reshape(1, -1), rows, wave.reshape(half, 2, syms, subs, k))
    )
    hbm = pl.BlockSpec(memory_space=pltpu.HBM)
    vmem = pl.BlockSpec(memory_space=pltpu.VMEM)
    params = pltpu.CompilerParams(vmem_limit_bytes=8 * 2**20)
    out = jax.ShapeDtypeStruct((half, syms, subs, c), jnp.bfloat16)
    blocks = pltpu.VMEM((half, syms, subs, k), jnp.bfloat16)
    given, matrix = pl.pallas_call(
        given_kernel,
        in_specs=[hbm] * 3,
        out_specs=[vmem] * 2,
        out_shape=[out, jax.ShapeDtypeStruct((k, c), jnp.bfloat16)],
        scratch_shapes=[
            blocks,
            pltpu.VMEM((1, n), jnp.int32),
            pltpu.VMEM((n, c), jnp.bfloat16),
            pltpu.SemaphoreType.DMA((COPIES + 2,)),
        ],
        compiler_params=params,
        name="given",
    )(lookup, rows, wave)
    kept, *facts = pl.pallas_call(
        kept_kernel,
        in_specs=[vmem] * 4 + [hbm],
        out_specs=[vmem] * 4,
        out_shape=[
            out,
            jax.ShapeDtypeStruct((PILOTS, pl.cdiv(syms, 8) * 8, c), jnp.float32),
            jax.ShapeDtypeStruct((subs, bits), jnp.float32),
            jax.ShapeDtypeStruct((2, subs, c), jnp.float32),
        ],
        scratch_shapes=[blocks, pltpu.SemaphoreType.DMA((COPIES,))],
        compiler_params=params,
        cost_estimate=pl.CostEstimate(
            flops=2 * half * syms * subs * k * c, bytes_accessed=2 * half * syms * subs * k, transcendentals=0
        ),
        name="kept",
    )(matrix, pilot_syms.reshape(1, -1), mod_order.reshape(1, -1), pilot_values, wave)
    return given, kept, facts


def entry(row, i):
    lane = lax.broadcasted_iota(jnp.int32, row.shape, 1)
    return jnp.sum(jnp.where(lane == i, row, 0.0), axis=1, keepdims=True)


def chosen_rows(chosen_ref, i, t, like):
    return jnp.broadcast_to(chosen_ref[i, t : t + 1, :], like.shape[-2:]) > 0.0


def as_column(row, count):
    diagonal = lax.broadcasted_iota(jnp.int32, (count, count), 0) == lax.broadcasted_iota(
        jnp.int32, (count, count), 1
    )
    return jnp.sum(jnp.where(diagonal, jnp.broadcast_to(row, (count, count)), 0.0), axis=1, keepdims=True)


def estimate_of(beams, pilot_re, pilot_im):
    c = beams.shape[-1]
    return beams * pilot_re + pltpu.roll(beams, c // 2, beams.ndim - 1) * pilot_im


def signed_pilots(pilot_ref, c):
    s = pilot_ref.shape[1]
    re = jnp.broadcast_to(as_column(pilot_ref[0:1, :], s), (s, c))
    im = jnp.broadcast_to(as_column(pilot_ref[1:2, :], s), (s, c))
    lane = lax.broadcasted_iota(jnp.int32, (s, c), 1)
    return re, jnp.where(lane < c // 2, im, -im)


def position():
    blocks = lax.axis_size(SUB)
    return lax.axis_index(PANEL) * blocks + lax.axis_index(SUB), lax.axis_size(PANEL) * blocks


def sum_kernel(chosen_ref, keep_ref, pilots_ref, parts_ref, *refs):
    *weights, own_ref, tail_ref, head_ref, llr_ref, patch_ref, wide_ref, even_ref, odd_ref = refs
    panels, syms, subs, c = parts_ref.shape

    def put(t, values):
        own_ref[t] = values
        head_ref[t] = values[:EDGE]
        tail_ref[t] = values[subs - EDGE :]

    at_pilots = [jnp.zeros((subs, c), jnp.float32) for _ in range(PILOTS)]
    for t in range(syms):
        total = parts_ref[0, t].astype(jnp.float32)
        for p in range(1, panels):
            total = total + parts_ref[p, t].astype(jnp.float32)
        beams = total.astype(jnp.bfloat16)
        put(t, beams)
        for i in range(PILOTS):
            at_pilots[i] = jnp.where(chosen_rows(chosen_ref, i, t, beams), beams.astype(jnp.float32), at_pilots[i])
    for i in range(PILOTS):
        put(syms + i, estimate_of(at_pilots[i], pilots_ref[0], pilots_ref[1]).astype(jnp.bfloat16))

    @pl.when(waits_long())
    def _():
        interior(chosen_ref, keep_ref, own_ref, *weights, llr_ref, patch_ref, wide_ref, even_ref, odd_ref)


def late_kernel(chosen_ref, keep_ref, own_ref, *refs):
    *weights, early_llr_ref, early_patch_ref, llr_ref, patch_ref, wide_ref, even_ref, odd_ref = refs
    del early_llr_ref, early_patch_ref

    @pl.when(jnp.logical_not(waits_long()))
    def _():
        interior(chosen_ref, keep_ref, own_ref, *weights, llr_ref, patch_ref, wide_ref, even_ref, odd_ref)


def waits_long():
    return lax.axis_index(SUB) < FIRST


def interior_shapes(syms, subs, c, layers, bits):
    return [
        jax.ShapeDtypeStruct((syms, subs, bits), jnp.float32),
        jax.ShapeDtypeStruct((layers - 1, syms, 2 * EDGE, c), jnp.float32),
    ]


def interior_scratch(syms, subs, c):
    padded = (syms + 2) * subs
    return [pltpu.VMEM((padded, lanes * c), jnp.bfloat16) for lanes in (2, 1, 1)]


def sum_beams(parts, facts, weights):
    _, syms, subs, c = parts.shape
    vmem = pl.BlockSpec(memory_space=pltpu.VMEM)
    edge = jax.ShapeDtypeStruct((syms + PILOTS, EDGE, c), jnp.bfloat16)
    layers, bits = weights[1].shape[0] + 1, weights[-1].shape[1]
    return pl.pallas_call(
        sum_kernel,
        in_specs=[vmem] * 10,
        out_specs=[vmem] * 5,
        out_shape=[
            jax.ShapeDtypeStruct((syms + PILOTS, subs, c), jnp.bfloat16),
            edge,
            edge,
            *interior_shapes(syms, subs, c, layers, bits),
        ],
        scratch_shapes=interior_scratch(syms, subs, c),
        compiler_params=pltpu.CompilerParams(vmem_limit_bytes=16 * 2**20),
        name="sum_beams",
    )(*facts, parts, *weights)


def pilot_rows(chosen_ref, rows, syms):
    spread = []
    for t in range(syms):
        row = jnp.zeros(rows.shape[1:], rows.dtype)
        for i in range(PILOTS):
            row = jnp.where(chosen_rows(chosen_ref, i, t, row), rows[i], row)
        spread.append(row)
    return jnp.stack(spread, 0)


def with_estimates(chosen_ref, pieces, syms):
    return jnp.concatenate([pieces[:syms], pilot_rows(chosen_ref, pieces[syms:], syms)], axis=2)


def taps_of(kernel, dt, dc):
    depth = kernel.shape[0] // 9
    return kernel[(3 * dt + dc) * depth : (3 * dt + dc + 1) * depth]


def demapped(field, in_ref, in_bias_ref, out_w_ref):
    hidden = jnp.dot(field, in_ref[...], preferred_element_type=jnp.float32)
    hidden = jnp.maximum(hidden + in_bias_ref[...], 0.0).astype(jnp.bfloat16)
    return jnp.dot(hidden, out_w_ref[...], preferred_element_type=jnp.float32)


def store_llr(ref, llr, keep, chosen_ref):
    rows = keep.shape[0]
    for t in range(ref.shape[0]):
        kept = keep > 0.0
        for i in range(PILOTS):
            kept = kept & jnp.logical_not(chosen_rows(chosen_ref, i, t, keep))
        ref[t] = jnp.where(kept, llr[t * rows : (t + 1) * rows], 0.0)


def interior(
    chosen_ref, keep_ref, own_ref, first_ref, rest_ref, bias_ref, in_ref, in_bias_ref, out_w_ref,
    llr_ref, patch_ref, wide_ref, even_ref, odd_ref,
):
    syms, subs, c = own_ref.shape
    syms = syms - PILOTS
    layers = rest_ref.shape[0] + 1
    rows = syms * subs
    for ref in (wide_ref, even_ref, odd_ref):
        ref[0:subs] = jnp.zeros((subs, ref.shape[1]), jnp.bfloat16)
        ref[subs + rows :] = jnp.zeros((subs, ref.shape[1]), jnp.bfloat16)
    wide_ref[subs : subs + rows, :c] = own_ref[:syms].reshape(rows, c)
    estimates = pilot_rows(chosen_ref, own_ref[syms:].astype(jnp.float32), syms)
    for t in range(syms):
        wide_ref[subs * (t + 1) : subs * (t + 2), c:] = estimates[t].astype(jnp.bfloat16)
    src = wide_ref
    for layer in range(1, layers + 1):
        kernel = first_ref[...] if layer == 1 else rest_ref[layer - 2]
        taps = jnp.concatenate([src[dt * subs : dt * subs + rows] for dt in range(3)], axis=1)
        wide = jnp.concatenate(
            [jnp.concatenate([taps_of(kernel, dt, dc) for dc in range(3)], axis=1) for dt in range(3)], axis=0
        )
        sums = jnp.dot(taps, wide, preferred_element_type=jnp.float32)
        total = sums[:, :c] + bias_ref[layer - 1 : layer, :]
        for dc in range(1, 3):
            total = total + pltpu.roll(sums[:, dc * c : (dc + 1) * c], rows - dc, 0)
        total = jnp.maximum(total, 0.0)
        if layer == layers:
            break
        src = (even_ref, odd_ref)[layer % 2]
        src[subs : subs + rows] = total.astype(jnp.bfloat16)
        spread = total.reshape(syms, subs, c)
        last = subs - 4 - 2 * layer
        group, place = last // EDGE * EDGE, last % EDGE
        high = spread[:, group : group + EDGE]
        if place != EDGE - 2:
            high = pltpu.roll(high, EDGE - 2 - place, 1)
        patch_ref[layer - 1] = jnp.concatenate([pltpu.roll(spread[:, :EDGE], EDGE - 2, 1), high], axis=1)
    final = pltpu.roll(total, layers, 0).astype(jnp.bfloat16)
    llr = demapped(final, in_ref, in_bias_ref, out_w_ref)
    store_llr(llr_ref, llr, keep_ref[...], chosen_ref)


def edge_kernel(
    chosen_ref, keep_ref, left_ref, right_ref, tail_ref, head_ref, patch_ref, inner_ref,
    first_ref, rest_ref, bias_ref, in_ref, in_bias_ref, out_w_ref,
    llr_ref, llr_buf, sems,
):
    syms, c = left_ref.shape[0] - PILOTS, left_ref.shape[2]
    layers = rest_ref.shape[0] + 1
    subs = llr_ref.shape[1]
    width = 2 * EDGE
    rows = syms * width
    middle = pl.ds(EDGE, subs - 2 * EDGE)
    inner_copy = pltpu.make_async_copy(inner_ref.at[:, middle], llr_ref.at[:, middle], sems.at[2])
    inner_copy.start()

    def joined(before, after, start):
        if start == 0:
            return before
        if start == EDGE:
            return after
        row = lax.broadcasted_iota(jnp.int32, before.shape, 1)
        turn = EDGE - start
        return jnp.where(row < turn, pltpu.roll(before, turn, 1), pltpu.roll(after, turn, 1))

    def convolved(shifted, kernel, bias):
        field = jnp.concatenate(shifted, axis=2)
        wide = jnp.concatenate(
            [jnp.concatenate([taps_of(kernel, dt, dc) for dt in range(3)], axis=1) for dc in range(3)], axis=0
        )
        sums = jnp.dot(
            field.reshape(syms * EDGE, field.shape[2]).astype(jnp.bfloat16), wide, preferred_element_type=jnp.float32
        ).reshape(syms, EDGE, 3 * c)
        nothing = jnp.zeros((1, EDGE, c), jnp.float32)
        total = sums[:, :, c : 2 * c] + bias[None]
        total = total + jnp.concatenate([nothing, sums[:-1, :, :c]], axis=0)
        total = total + jnp.concatenate([sums[1:, :, 2 * c :], nothing], axis=0)
        return jnp.maximum(total, 0.0)

    at, blocks = position()
    left, right, tail, head = (ref[...].astype(jnp.float32) for ref in (left_ref, right_ref, tail_ref, head_ref))
    fields = [
        [with_estimates(chosen_ref, joined(*ends, start + dc), syms) for dc in range(3)]
        for ends, start in (((left, head), EDGE - layers), ((tail, right), EDGE - 4))
    ]
    low, high = (convolved(field, first_ref[...], bias_ref[0:1, :]) for field in fields)
    row = lax.broadcasted_iota(jnp.int32, (EDGE, c), 0)
    for layer in range(1, layers):
        low = jnp.where(((row < layers - layer) & (at == 0))[None], 0.0, low)
        high = jnp.where(((row >= 2 + layer) & (at == blocks - 1))[None], 0.0, high)
        patch = patch_ref[layer - 1]
        fields = [
            [joined(low, patch[:, :EDGE], dc) for dc in range(3)],
            [joined(patch[:, EDGE:], high, EDGE - 2 + dc) for dc in range(3)],
        ]
        low, high = (convolved(field, rest_ref[layer - 1], bias_ref[layer : layer + 1, :]) for field in fields)
    total = jnp.concatenate([low, high], axis=1)
    llr = demapped(total.reshape(rows, c).astype(jnp.bfloat16), in_ref, in_bias_ref, out_w_ref)
    keep = jnp.concatenate([keep_ref[:EDGE], keep_ref[subs - EDGE :]], axis=0)
    store_llr(llr_buf, llr, keep, chosen_ref)
    copies = [
        pltpu.make_async_copy(
            llr_buf.at[:, pl.ds(side * EDGE, EDGE)], llr_ref.at[:, pl.ds(start, EDGE)], sems.at[side]
        )
        for side, start in enumerate((0, subs - EDGE))
    ]
    for copy in copies:
        copy.start()
    inner_copy.wait()
    for copy in copies:
        copy.wait()


def receive_interior(facts, own, weights, early):
    syms, subs, c = own.shape
    syms = syms - PILOTS
    layers, bits = weights[1].shape[0] + 1, weights[-1].shape[1]
    vmem = pl.BlockSpec(memory_space=pltpu.VMEM)
    return pl.pallas_call(
        late_kernel,
        in_specs=[vmem] * 11,
        out_specs=[vmem] * 2,
        out_shape=interior_shapes(syms, subs, c, layers, bits),
        input_output_aliases={9: 0, 10: 1},
        scratch_shapes=interior_scratch(syms, subs, c),
        compiler_params=pltpu.CompilerParams(vmem_limit_bytes=16 * 2**20),
        cost_estimate=pl.CostEstimate(flops=10**9, bytes_accessed=4 * 10**6, transcendentals=0),
        name="interior",
    )(*facts[:2], own, *weights, *early)


def receive_edges(facts, got, sent, patch, weights, inner):
    syms, subs, bits = inner.shape
    vmem = pl.BlockSpec(memory_space=pltpu.VMEM)
    return pl.pallas_call(
        edge_kernel,
        in_specs=[vmem] * 14,
        out_specs=pl.BlockSpec(memory_space=pltpu.HBM),
        out_shape=pltpu.HBM(inner.shape, jnp.float32),
        scratch_shapes=[
            pltpu.VMEM((syms, 2 * EDGE, bits), jnp.float32),
            pltpu.SemaphoreType.DMA((3,)),
        ],
        compiler_params=pltpu.CompilerParams(vmem_limit_bytes=16 * 2**20),
        cost_estimate=pl.CostEstimate(flops=5 * 10**8, bytes_accessed=4 * 10**6, transcendentals=0),
        name="edges",
    )(*facts[:2], *got, *sent, patch, inner, *weights)


def per_device(
    captured_waveform,
    element_lookup,
    combiner,
    pilot_syms,
    pilot_values,
    mod_order,
    conv_first,
    conv_rest,
    conv_bias,
    demap_in,
    demap_bias,
    demap_out,
):
    given, kept, facts = beam_partials(
        captured_waveform, element_lookup, combiner, pilot_syms, mod_order, pilot_values, demap_out.shape[1]
    )
    panels = lax.axis_size(PANEL)
    got = lax.ppermute(given, PANEL, [(p, p ^ 1) for p in range(panels)])
    pairs = (kept.astype(jnp.float32) + got.astype(jnp.float32)).astype(jnp.bfloat16)
    same_core = [list(range(core, panels, 2)) for core in range(2)]
    parts = lax.all_to_all(pairs, PANEL, 0, 0, axis_index_groups=same_core, tiled=True)
    c = combiner.shape[1]
    weights = (
        conv_first.reshape(-1, c),
        conv_rest.reshape(conv_rest.shape[0], -1, c),
        conv_bias,
        demap_in,
        demap_bias.reshape(1, -1),
        demap_out,
    )
    own, tail, head, *early = sum_beams(parts, facts, weights)
    both = (PANEL, SUB)
    count = lax.axis_size(both)
    left = lax.ppermute(tail, both, [(i, i + 1) for i in range(count - 1)])
    right = lax.ppermute(head, both, [(i + 1, i) for i in range(count - 1)])
    inner, patch = receive_interior(facts, own, weights, early)
    return receive_edges(facts, (left, right), (tail, head), patch, weights, inner)


def solution(mesh):
    in_specs = (
        P(None, None, SUB, PANEL),
        P(PANEL),
        P(PANEL, None),
        P(),
        P(None, (PANEL, SUB)),
        P((PANEL, SUB)),
        P(),
        P(),
        P(),
        P(),
        P(),
        P(),
    )
    out_specs = P(None, (PANEL, SUB), None)
    return jax.shard_map(
        per_device, mesh=mesh, in_specs=in_specs, out_specs=out_specs, check_vma=False
    )
```

```python
import jax
import jax.numpy as jnp
from jax import lax
from jax.experimental import pallas as pl
from jax.experimental.pallas import tpu as pltpu
from jax.sharding import PartitionSpec as P

RB_SC = 4
BITS = 8
PILOTS = 2
COPIES = 4
FIRST = 1
EDGE = 8
PANEL = "panel"
SUB = "sc"


def lookup_matrix(lookup, rows):
    n, c = rows.shape
    member = lax.broadcasted_iota(jnp.int32, (n, n), 0) == lookup % n
    picked = lax.dot_general(
        member.astype(jnp.bfloat16), rows, (((0,), (0,)), ((), ())), preferred_element_type=jnp.float32
    ).astype(jnp.bfloat16)
    doubled = (
        lax.broadcasted_iota(jnp.int32, (2 * n, n), 0) // 2 == lax.broadcasted_iota(jnp.int32, (2 * n, n), 1)
    )
    w = jnp.dot(doubled.astype(jnp.bfloat16), picked, preferred_element_type=jnp.float32)
    lane = lax.broadcasted_iota(jnp.int32, w.shape, 1)
    turned = pltpu.roll(w, c // 2, 1) * jnp.where(lane < c // 2, -1.0, 1.0)
    odd = lax.broadcasted_iota(jnp.int32, w.shape, 0) % 2 == 1
    return jnp.where(odd, turned, w).astype(jnp.bfloat16)


def matrix_kernel_body(wave_ref, out_ref, blocks_ref, sems, matrix, parity):
    count, syms, subs, c = out_ref.shape
    k = wave_ref.shape[4]
    step = count // COPIES

    def fetch(i):
        some = pl.ds(i * step, step)
        return pltpu.make_async_copy(wave_ref.at[some, parity], blocks_ref.at[some], sems.at[i])

    for i in range(COPIES):
        fetch(i).start()
    weights = matrix()
    for first, last in ((0, step), (step, count)):
        for i in range(first // step, last // step):
            fetch(i).wait()
        lines = blocks_ref[first:last].reshape((last - first) * syms * subs, k)
        out_ref[first:last] = (
            jnp.dot(lines, weights, preferred_element_type=jnp.float32)
            .astype(jnp.bfloat16)
            .reshape(last - first, syms, subs, c)
        )


def given_kernel(lookup_ref, rows_ref, wave_ref, out_ref, matrix_ref, blocks_ref, lookup_buf, rows_buf, sems):
    copies = [
        pltpu.make_async_copy(lookup_ref, lookup_buf, sems.at[COPIES]),
        pltpu.make_async_copy(rows_ref, rows_buf, sems.at[COPIES + 1]),
    ]
    for copy in copies:
        copy.start()

    def matrix():
        for copy in copies:
            copy.wait()
        matrix_ref[...] = lookup_matrix(lookup_buf[...], rows_buf[...])
        return matrix_ref[...]

    parity = 1 - lax.axis_index(PANEL) % 2
    matrix_kernel_body(wave_ref, out_ref, blocks_ref, sems, matrix, parity)


def kept_kernel(
    matrix_ref, syms_ref, order_ref, pilot_ref, wave_ref, out_ref, chosen_ref, keep_ref, pilots_ref, blocks_ref, sems
):
    def matrix():
        for i in range(PILOTS):
            at = jnp.broadcast_to(entry(syms_ref[...].astype(jnp.float32), i), chosen_ref.shape[1:])
            row = lax.broadcasted_iota(jnp.int32, chosen_ref.shape[1:], 0)
            chosen_ref[i] = jnp.where(row.astype(jnp.float32) == at, 1.0, 0.0)
        subs, bits = keep_ref.shape
        blocks = order_ref.shape[1]
        mine = lax.broadcasted_iota(jnp.int32, (subs, blocks), 0) // RB_SC == lax.broadcasted_iota(
            jnp.int32, (subs, blocks), 1
        )
        orders = jnp.broadcast_to(order_ref[...].astype(jnp.float32), (subs, blocks))
        limit = 2.0 * jnp.sum(jnp.where(mine, orders, 0.0), axis=1, keepdims=True)
        bit = lax.broadcasted_iota(jnp.int32, (subs, bits), 1) % BITS
        keep_ref[...] = jnp.where(bit.astype(jnp.float32) < limit, 1.0, 0.0)
        pilots_ref[0], pilots_ref[1] = signed_pilots(pilot_ref, pilots_ref.shape[2])
        return matrix_ref[...]

    parity = lax.axis_index(PANEL) % 2
    matrix_kernel_body(wave_ref, out_ref, blocks_ref, sems, matrix, parity)


def beam_partials(wave, lookup, rows, pilot_syms, mod_order, pilot_values, bits):
    groups, syms, subs, k = wave.shape
    n, c = rows.shape
    half = groups // 2
    lookup, rows, wave = (
        pltpu.with_memory_space_constraint(array, pltpu.HBM)
        for array in (lookup.reshape(1, -1), rows, wave.reshape(half, 2, syms, subs, k))
    )
    hbm = pl.BlockSpec(memory_space=pltpu.HBM)
    vmem = pl.BlockSpec(memory_space=pltpu.VMEM)
    params = pltpu.CompilerParams(vmem_limit_bytes=8 * 2**20)
    out = jax.ShapeDtypeStruct((half, syms, subs, c), jnp.bfloat16)
    blocks = pltpu.VMEM((half, syms, subs, k), jnp.bfloat16)
    given, matrix = pl.pallas_call(
        given_kernel,
        in_specs=[hbm] * 3,
        out_specs=[vmem] * 2,
        out_shape=[out, jax.ShapeDtypeStruct((k, c), jnp.bfloat16)],
        scratch_shapes=[
            blocks,
            pltpu.VMEM((1, n), jnp.int32),
            pltpu.VMEM((n, c), jnp.bfloat16),
            pltpu.SemaphoreType.DMA((COPIES + 2,)),
        ],
        compiler_params=params,
        name="given",
    )(lookup, rows, wave)
    kept, *facts = pl.pallas_call(
        kept_kernel,
        in_specs=[vmem] * 4 + [hbm],
        out_specs=[vmem] * 4,
        out_shape=[
            out,
            jax.ShapeDtypeStruct((PILOTS, pl.cdiv(syms, 8) * 8, c), jnp.float32),
            jax.ShapeDtypeStruct((subs, bits), jnp.float32),
            jax.ShapeDtypeStruct((2, subs, c), jnp.float32),
        ],
        scratch_shapes=[blocks, pltpu.SemaphoreType.DMA((COPIES,))],
        compiler_params=params,
        cost_estimate=pl.CostEstimate(
            flops=2 * half * syms * subs * k * c, bytes_accessed=2 * half * syms * subs * k, transcendentals=0
        ),
        name="kept",
    )(matrix, pilot_syms.reshape(1, -1), mod_order.reshape(1, -1), pilot_values, wave)
    return given, kept, facts


def entry(row, i):
    lane = lax.broadcasted_iota(jnp.int32, row.shape, 1)
    return jnp.sum(jnp.where(lane == i, row, 0.0), axis=1, keepdims=True)


def chosen_rows(chosen_ref, i, t, like):
    return jnp.broadcast_to(chosen_ref[i, t : t + 1, :], like.shape[-2:]) > 0.0


def as_column(row, count):
    diagonal = lax.broadcasted_iota(jnp.int32, (count, count), 0) == lax.broadcasted_iota(
        jnp.int32, (count, count), 1
    )
    return jnp.sum(jnp.where(diagonal, jnp.broadcast_to(row, (count, count)), 0.0), axis=1, keepdims=True)


def estimate_of(beams, pilot_re, pilot_im):
    c = beams.shape[-1]
    return beams * pilot_re + pltpu.roll(beams, c // 2, beams.ndim - 1) * pilot_im


def signed_pilots(pilot_ref, c):
    s = pilot_ref.shape[1]
    re = jnp.broadcast_to(as_column(pilot_ref[0:1, :], s), (s, c))
    im = jnp.broadcast_to(as_column(pilot_ref[1:2, :], s), (s, c))
    lane = lax.broadcasted_iota(jnp.int32, (s, c), 1)
    return re, jnp.where(lane < c // 2, im, -im)


def position():
    blocks = lax.axis_size(SUB)
    return lax.axis_index(PANEL) * blocks + lax.axis_index(SUB), lax.axis_size(PANEL) * blocks


def sum_kernel(chosen_ref, keep_ref, pilots_ref, parts_ref, *refs):
    *weights, own_ref, tail_ref, head_ref, llr_ref, patch_ref, wide_ref, even_ref, odd_ref = refs
    panels, syms, subs, c = parts_ref.shape

    def put(t, values):
        own_ref[t] = values
        head_ref[t] = values[:EDGE]
        tail_ref[t] = values[subs - EDGE :]

    at_pilots = [jnp.zeros((subs, c), jnp.float32) for _ in range(PILOTS)]
    for t in range(syms):
        total = parts_ref[0, t].astype(jnp.float32)
        for p in range(1, panels):
            total = total + parts_ref[p, t].astype(jnp.float32)
        beams = total.astype(jnp.bfloat16)
        put(t, beams)
        for i in range(PILOTS):
            at_pilots[i] = jnp.where(chosen_rows(chosen_ref, i, t, beams), beams.astype(jnp.float32), at_pilots[i])
    for i in range(PILOTS):
        put(syms + i, estimate_of(at_pilots[i], pilots_ref[0], pilots_ref[1]).astype(jnp.bfloat16))

    @pl.when(waits_long())
    def _():
        interior(chosen_ref, keep_ref, own_ref, *weights, llr_ref, patch_ref, wide_ref, even_ref, odd_ref)


def late_kernel(chosen_ref, keep_ref, own_ref, *refs):
    *weights, early_llr_ref, early_patch_ref, llr_ref, patch_ref, wide_ref, even_ref, odd_ref = refs
    del early_llr_ref, early_patch_ref

    @pl.when(jnp.logical_not(waits_long()))
    def _():
        interior(chosen_ref, keep_ref, own_ref, *weights, llr_ref, patch_ref, wide_ref, even_ref, odd_ref)


def waits_long():
    return lax.axis_index(SUB) < FIRST


def interior_shapes(syms, subs, c, layers, bits):
    return [
        jax.ShapeDtypeStruct((syms, subs, bits), jnp.float32),
        jax.ShapeDtypeStruct((layers - 1, syms, 2 * EDGE, c), jnp.float32),
    ]


def interior_scratch(syms, subs, c):
    padded = (syms + 2) * subs
    return [pltpu.VMEM((padded, lanes * c), jnp.bfloat16) for lanes in (2, 1, 1)]


def sum_beams(parts, facts, weights):
    _, syms, subs, c = parts.shape
    vmem = pl.BlockSpec(memory_space=pltpu.VMEM)
    edge = jax.ShapeDtypeStruct((syms + PILOTS, EDGE, c), jnp.bfloat16)
    layers, bits = weights[1].shape[0] + 1, weights[-1].shape[1]
    return pl.pallas_call(
        sum_kernel,
        in_specs=[vmem] * 10,
        out_specs=[vmem] * 5,
        out_shape=[
            jax.ShapeDtypeStruct((syms + PILOTS, subs, c), jnp.bfloat16),
            edge,
            edge,
            *interior_shapes(syms, subs, c, layers, bits),
        ],
        scratch_shapes=interior_scratch(syms, subs, c),
        compiler_params=pltpu.CompilerParams(vmem_limit_bytes=16 * 2**20),
        name="sum_beams",
    )(*facts, parts, *weights)


def pilot_rows(chosen_ref, rows, syms):
    spread = []
    for t in range(syms):
        row = jnp.zeros(rows.shape[1:], rows.dtype)
        for i in range(PILOTS):
            row = jnp.where(chosen_rows(chosen_ref, i, t, row), rows[i], row)
        spread.append(row)
    return jnp.stack(spread, 0)


def with_estimates(chosen_ref, pieces, syms):
    return jnp.concatenate([pieces[:syms], pilot_rows(chosen_ref, pieces[syms:], syms)], axis=2)


def taps_of(kernel, dt, dc):
    depth = kernel.shape[0] // 9
    return kernel[(3 * dt + dc) * depth : (3 * dt + dc + 1) * depth]


def demapped(field, in_ref, in_bias_ref, out_w_ref):
    hidden = jnp.dot(field, in_ref[...], preferred_element_type=jnp.float32)
    hidden = jnp.maximum(hidden + in_bias_ref[...], 0.0).astype(jnp.bfloat16)
    return jnp.dot(hidden, out_w_ref[...], preferred_element_type=jnp.float32)


def store_llr(ref, llr, keep, chosen_ref):
    rows = keep.shape[0]
    for t in range(ref.shape[0]):
        kept = keep > 0.0
        for i in range(PILOTS):
            kept = kept & jnp.logical_not(chosen_rows(chosen_ref, i, t, keep))
        ref[t] = jnp.where(kept, llr[t * rows : (t + 1) * rows], 0.0)


def interior(
    chosen_ref, keep_ref, own_ref, first_ref, rest_ref, bias_ref, in_ref, in_bias_ref, out_w_ref,
    llr_ref, patch_ref, wide_ref, even_ref, odd_ref,
):
    syms, subs, c = own_ref.shape
    syms = syms - PILOTS
    layers = rest_ref.shape[0] + 1
    rows = syms * subs
    for ref in (wide_ref, even_ref, odd_ref):
        ref[0:subs] = jnp.zeros((subs, ref.shape[1]), jnp.bfloat16)
        ref[subs + rows :] = jnp.zeros((subs, ref.shape[1]), jnp.bfloat16)
    wide_ref[subs : subs + rows, :c] = own_ref[:syms].reshape(rows, c)
    estimates = pilot_rows(chosen_ref, own_ref[syms:].astype(jnp.float32), syms)
    for t in range(syms):
        wide_ref[subs * (t + 1) : subs * (t + 2), c:] = estimates[t].astype(jnp.bfloat16)
    src = wide_ref
    for layer in range(1, layers + 1):
        kernel = first_ref[...] if layer == 1 else rest_ref[layer - 2]
        taps = jnp.concatenate([src[dt * subs : dt * subs + rows] for dt in range(3)], axis=1)
        wide = jnp.concatenate(
            [jnp.concatenate([taps_of(kernel, dt, dc) for dc in range(3)], axis=1) for dt in range(3)], axis=0
        )
        sums = jnp.dot(taps, wide, preferred_element_type=jnp.float32)
        total = sums[:, :c] + bias_ref[layer - 1 : layer, :]
        for dc in range(1, 3):
            total = total + pltpu.roll(sums[:, dc * c : (dc + 1) * c], rows - dc, 0)
        total = jnp.maximum(total, 0.0)
        if layer == layers:
            break
        src = (even_ref, odd_ref)[layer % 2]
        src[subs : subs + rows] = total.astype(jnp.bfloat16)
        spread = total.reshape(syms, subs, c)
        last = subs - 4 - 2 * layer
        group, place = last // EDGE * EDGE, last % EDGE
        high = spread[:, group : group + EDGE]
        if place != EDGE - 2:
            high = pltpu.roll(high, EDGE - 2 - place, 1)
        patch_ref[layer - 1] = jnp.concatenate([pltpu.roll(spread[:, :EDGE], EDGE - 2, 1), high], axis=1)
    final = pltpu.roll(total, layers, 0).astype(jnp.bfloat16)
    llr = demapped(final, in_ref, in_bias_ref, out_w_ref)
    store_llr(llr_ref, llr, keep_ref[...], chosen_ref)


def edge_kernel(
    chosen_ref, keep_ref, left_ref, right_ref, tail_ref, head_ref, patch_ref, inner_ref,
    first_ref, rest_ref, bias_ref, in_ref, in_bias_ref, out_w_ref,
    llr_ref, llr_buf, sems,
):
    syms, c = left_ref.shape[0] - PILOTS, left_ref.shape[2]
    layers = rest_ref.shape[0] + 1
    subs = llr_ref.shape[1]
    width = 2 * EDGE
    rows = syms * width
    middle = pl.ds(EDGE, subs - 2 * EDGE)
    inner_copy = pltpu.make_async_copy(inner_ref.at[:, middle], llr_ref.at[:, middle], sems.at[2])
    inner_copy.start()

    def joined(before, after, start):
        if start == 0:
            return before
        if start == EDGE:
            return after
        row = lax.broadcasted_iota(jnp.int32, before.shape, 1)
        turn = EDGE - start
        return jnp.where(row < turn, pltpu.roll(before, turn, 1), pltpu.roll(after, turn, 1))

    def convolved(shifted, kernel, bias):
        field = jnp.concatenate(shifted, axis=2)
        wide = jnp.concatenate(
            [jnp.concatenate([taps_of(kernel, dt, dc) for dt in range(3)], axis=1) for dc in range(3)], axis=0
        )
        sums = jnp.dot(
            field.reshape(syms * EDGE, field.shape[2]).astype(jnp.bfloat16), wide, preferred_element_type=jnp.float32
        ).reshape(syms, EDGE, 3 * c)
        nothing = jnp.zeros((1, EDGE, c), jnp.float32)
        total = sums[:, :, c : 2 * c] + bias[None]
        total = total + jnp.concatenate([nothing, sums[:-1, :, :c]], axis=0)
        total = total + jnp.concatenate([sums[1:, :, 2 * c :], nothing], axis=0)
        return jnp.maximum(total, 0.0)

    at, blocks = position()
    left, right, tail, head = (ref[...].astype(jnp.float32) for ref in (left_ref, right_ref, tail_ref, head_ref))
    fields = [
        [with_estimates(chosen_ref, joined(*ends, start + dc), syms) for dc in range(3)]
        for ends, start in (((left, head), EDGE - layers), ((tail, right), EDGE - 4))
    ]
    low, high = (convolved(field, first_ref[...], bias_ref[0:1, :]) for field in fields)
    row = lax.broadcasted_iota(jnp.int32, (EDGE, c), 0)
    for layer in range(1, layers):
        low = jnp.where(((row < layers - layer) & (at == 0))[None], 0.0, low)
        high = jnp.where(((row >= 2 + layer) & (at == blocks - 1))[None], 0.0, high)
        patch = patch_ref[layer - 1]
        fields = [
            [joined(low, patch[:, :EDGE], dc) for dc in range(3)],
            [joined(patch[:, EDGE:], high, EDGE - 2 + dc) for dc in range(3)],
        ]
        low, high = (convolved(field, rest_ref[layer - 1], bias_ref[layer : layer + 1, :]) for field in fields)
    copies = []
    for side, (field, start) in enumerate(((low, 0), (high, subs - EDGE))):
        llr = demapped(field.reshape(syms * EDGE, c).astype(jnp.bfloat16), in_ref, in_bias_ref, out_w_ref)
        store_llr(llr_buf.at[side], llr, keep_ref[start : start + EDGE], chosen_ref)
        copy = pltpu.make_async_copy(llr_buf.at[side], llr_ref.at[:, pl.ds(start, EDGE)], sems.at[side])
        copy.start()
        copies.append(copy)
    inner_copy.wait()
    for copy in copies:
        copy.wait()


def receive_interior(facts, own, weights, early):
    syms, subs, c = own.shape
    syms = syms - PILOTS
    layers, bits = weights[1].shape[0] + 1, weights[-1].shape[1]
    vmem = pl.BlockSpec(memory_space=pltpu.VMEM)
    return pl.pallas_call(
        late_kernel,
        in_specs=[vmem] * 11,
        out_specs=[vmem] * 2,
        out_shape=interior_shapes(syms, subs, c, layers, bits),
        input_output_aliases={9: 0, 10: 1},
        scratch_shapes=interior_scratch(syms, subs, c),
        compiler_params=pltpu.CompilerParams(vmem_limit_bytes=16 * 2**20),
        cost_estimate=pl.CostEstimate(flops=10**9, bytes_accessed=4 * 10**6, transcendentals=0),
        name="interior",
    )(*facts[:2], own, *weights, *early)


def receive_edges(facts, got, sent, patch, weights, inner):
    syms, subs, bits = inner.shape
    vmem = pl.BlockSpec(memory_space=pltpu.VMEM)
    return pl.pallas_call(
        edge_kernel,
        in_specs=[vmem] * 14,
        out_specs=pl.BlockSpec(memory_space=pltpu.HBM),
        out_shape=pltpu.HBM(inner.shape, jnp.float32),
        scratch_shapes=[
            pltpu.VMEM((2, syms, EDGE, bits), jnp.float32),
            pltpu.SemaphoreType.DMA((3,)),
        ],
        compiler_params=pltpu.CompilerParams(vmem_limit_bytes=16 * 2**20),
        cost_estimate=pl.CostEstimate(flops=5 * 10**8, bytes_accessed=4 * 10**6, transcendentals=0),
        name="edges",
    )(*facts[:2], *got, *sent, patch, inner, *weights)


def per_device(
    captured_waveform,
    element_lookup,
    combiner,
    pilot_syms,
    pilot_values,
    mod_order,
    conv_first,
    conv_rest,
    conv_bias,
    demap_in,
    demap_bias,
    demap_out,
):
    given, kept, facts = beam_partials(
        captured_waveform, element_lookup, combiner, pilot_syms, mod_order, pilot_values, demap_out.shape[1]
    )
    panels = lax.axis_size(PANEL)
    got = lax.ppermute(given, PANEL, [(p, p ^ 1) for p in range(panels)])
    pairs = (kept.astype(jnp.float32) + got.astype(jnp.float32)).astype(jnp.bfloat16)
    same_core = [list(range(core, panels, 2)) for core in range(2)]
    parts = lax.all_to_all(pairs, PANEL, 0, 0, axis_index_groups=same_core, tiled=True)
    c = combiner.shape[1]
    weights = (
        conv_first.reshape(-1, c),
        conv_rest.reshape(conv_rest.shape[0], -1, c),
        conv_bias,
        demap_in,
        demap_bias.reshape(1, -1),
        demap_out,
    )
    own, tail, head, *early = sum_beams(parts, facts, weights)
    both = (PANEL, SUB)
    count = lax.axis_size(both)
    left = lax.ppermute(tail, both, [(i, i + 1) for i in range(count - 1)])
    right = lax.ppermute(head, both, [(i + 1, i) for i in range(count - 1)])
    inner, patch = receive_interior(facts, own, weights, early)
    return receive_edges(facts, (left, right), (tail, head), patch, weights, inner)


def solution(mesh):
    in_specs = (
        P(None, None, SUB, PANEL),
        P(PANEL),
        P(PANEL, None),
        P(),
        P(None, (PANEL, SUB)),
        P((PANEL, SUB)),
        P(),
        P(),
        P(),
        P(),
        P(),
        P(),
    )
    out_specs = P(None, (PANEL, SUB), None)
    return jax.shard_map(
        per_device, mesh=mesh, in_specs=in_specs, out_specs=out_specs, check_vma=False
    )
```

```python
import jax
import jax.numpy as jnp
from jax import lax
from jax.experimental import pallas as pl
from jax.experimental.pallas import tpu as pltpu
from jax.sharding import PartitionSpec as P

RB_SC = 4
BITS = 8
PILOTS = 2
COPIES = 4
FIRST = 1
EDGE = 8
PANEL = "panel"
SUB = "sc"


def lookup_matrix(lookup, rows):
    n, c = rows.shape
    member = lax.broadcasted_iota(jnp.int32, (n, n), 0) == lookup % n
    picked = lax.dot_general(
        member.astype(jnp.bfloat16), rows, (((0,), (0,)), ((), ())), preferred_element_type=jnp.float32
    ).astype(jnp.bfloat16)
    doubled = (
        lax.broadcasted_iota(jnp.int32, (2 * n, n), 0) // 2 == lax.broadcasted_iota(jnp.int32, (2 * n, n), 1)
    )
    w = jnp.dot(doubled.astype(jnp.bfloat16), picked, preferred_element_type=jnp.float32)
    lane = lax.broadcasted_iota(jnp.int32, w.shape, 1)
    turned = pltpu.roll(w, c // 2, 1) * jnp.where(lane < c // 2, -1.0, 1.0)
    odd = lax.broadcasted_iota(jnp.int32, w.shape, 0) % 2 == 1
    return jnp.where(odd, turned, w).astype(jnp.bfloat16)


def matrix_kernel_body(wave_ref, out_ref, blocks_ref, sems, matrix, parity):
    count, syms, subs, c = out_ref.shape
    k = wave_ref.shape[4]
    step = count // COPIES

    def fetch(i):
        some = pl.ds(i * step, step)
        return pltpu.make_async_copy(wave_ref.at[some, parity], blocks_ref.at[some], sems.at[i])

    for i in range(COPIES):
        fetch(i).start()
    weights = matrix()
    for first, last in ((0, step), (step, count)):
        for i in range(first // step, last // step):
            fetch(i).wait()
        lines = blocks_ref[first:last].reshape((last - first) * syms * subs, k)
        out_ref[first:last] = (
            jnp.dot(lines, weights, preferred_element_type=jnp.float32)
            .astype(jnp.bfloat16)
            .reshape(last - first, syms, subs, c)
        )


def given_kernel(lookup_ref, rows_ref, wave_ref, out_ref, matrix_ref, blocks_ref, lookup_buf, rows_buf, sems):
    copies = [
        pltpu.make_async_copy(lookup_ref, lookup_buf, sems.at[COPIES]),
        pltpu.make_async_copy(rows_ref, rows_buf, sems.at[COPIES + 1]),
    ]
    for copy in copies:
        copy.start()

    def matrix():
        for copy in copies:
            copy.wait()
        matrix_ref[...] = lookup_matrix(lookup_buf[...], rows_buf[...])
        return matrix_ref[...]

    parity = 1 - lax.axis_index(PANEL) % 2
    matrix_kernel_body(wave_ref, out_ref, blocks_ref, sems, matrix, parity)


def kept_kernel(
    matrix_ref, syms_ref, order_ref, pilot_ref, wave_ref, out_ref, chosen_ref, keep_ref, pilots_ref, blocks_ref, sems
):
    def matrix():
        for i in range(PILOTS):
            at = jnp.broadcast_to(entry(syms_ref[...].astype(jnp.float32), i), chosen_ref.shape[1:])
            row = lax.broadcasted_iota(jnp.int32, chosen_ref.shape[1:], 0)
            chosen_ref[i] = jnp.where(row.astype(jnp.float32) == at, 1.0, 0.0)
        subs, bits = keep_ref.shape
        blocks = order_ref.shape[1]
        mine = lax.broadcasted_iota(jnp.int32, (subs, blocks), 0) // RB_SC == lax.broadcasted_iota(
            jnp.int32, (subs, blocks), 1
        )
        orders = jnp.broadcast_to(order_ref[...].astype(jnp.float32), (subs, blocks))
        limit = 2.0 * jnp.sum(jnp.where(mine, orders, 0.0), axis=1, keepdims=True)
        bit = lax.broadcasted_iota(jnp.int32, (subs, bits), 1) % BITS
        keep_ref[...] = jnp.where(bit.astype(jnp.float32) < limit, 1.0, 0.0)
        pilots_ref[0], pilots_ref[1] = signed_pilots(pilot_ref, pilots_ref.shape[2])
        return matrix_ref[...]

    weights = matrix()

    @pl.when(first_to_exchange())
    def _():
        matrix_kernel_body(wave_ref, out_ref, blocks_ref, sems, lambda: weights, lax.axis_index(PANEL) % 2)


def first_to_exchange():
    return lax.axis_index(PANEL) % 2 == 0


def pair_kernel(matrix_ref, kept_ref, got_ref, wave_ref, out_ref, blocks_ref, sems):
    @pl.when(first_to_exchange())
    def _():
        out_ref[...] = (kept_ref[...].astype(jnp.float32) + got_ref[...].astype(jnp.float32)).astype(jnp.bfloat16)

    @pl.when(jnp.logical_not(first_to_exchange()))
    def _():
        matrix_kernel_body(
            wave_ref, out_ref, blocks_ref, sems, lambda: matrix_ref[...], lax.axis_index(PANEL) % 2
        )
        out_ref[...] = (out_ref[...].astype(jnp.float32) + got_ref[...].astype(jnp.float32)).astype(jnp.bfloat16)


def pair_sums(matrix, kept, got, wave):
    half, syms, subs, _ = kept.shape
    k = wave.shape[3]
    vmem = pl.BlockSpec(memory_space=pltpu.VMEM)
    wave = pltpu.with_memory_space_constraint(wave.reshape(half, 2, syms, subs, k), pltpu.HBM)
    return pl.pallas_call(
        pair_kernel,
        in_specs=[vmem] * 3 + [pl.BlockSpec(memory_space=pltpu.HBM)],
        out_specs=vmem,
        out_shape=jax.ShapeDtypeStruct(kept.shape, kept.dtype),
        scratch_shapes=[pltpu.VMEM((half, syms, subs, k), jnp.bfloat16), pltpu.SemaphoreType.DMA((COPIES,))],
        compiler_params=pltpu.CompilerParams(vmem_limit_bytes=8 * 2**20),
        name="pair_sums",
    )(matrix, kept, got, wave)


def beam_partials(wave, lookup, rows, pilot_syms, mod_order, pilot_values, bits):
    groups, syms, subs, k = wave.shape
    n, c = rows.shape
    half = groups // 2
    lookup, rows, wave = (
        pltpu.with_memory_space_constraint(array, pltpu.HBM)
        for array in (lookup.reshape(1, -1), rows, wave.reshape(half, 2, syms, subs, k))
    )
    hbm = pl.BlockSpec(memory_space=pltpu.HBM)
    vmem = pl.BlockSpec(memory_space=pltpu.VMEM)
    params = pltpu.CompilerParams(vmem_limit_bytes=8 * 2**20)
    out = jax.ShapeDtypeStruct((half, syms, subs, c), jnp.bfloat16)
    blocks = pltpu.VMEM((half, syms, subs, k), jnp.bfloat16)
    given, matrix = pl.pallas_call(
        given_kernel,
        in_specs=[hbm] * 3,
        out_specs=[vmem] * 2,
        out_shape=[out, jax.ShapeDtypeStruct((k, c), jnp.bfloat16)],
        scratch_shapes=[
            blocks,
            pltpu.VMEM((1, n), jnp.int32),
            pltpu.VMEM((n, c), jnp.bfloat16),
            pltpu.SemaphoreType.DMA((COPIES + 2,)),
        ],
        compiler_params=params,
        name="given",
    )(lookup, rows, wave)
    kept, *facts = pl.pallas_call(
        kept_kernel,
        in_specs=[vmem] * 4 + [hbm],
        out_specs=[vmem] * 4,
        out_shape=[
            out,
            jax.ShapeDtypeStruct((PILOTS, pl.cdiv(syms, 8) * 8, c), jnp.float32),
            jax.ShapeDtypeStruct((subs, bits), jnp.float32),
            jax.ShapeDtypeStruct((2, subs, c), jnp.float32),
        ],
        scratch_shapes=[blocks, pltpu.SemaphoreType.DMA((COPIES,))],
        compiler_params=params,
        cost_estimate=pl.CostEstimate(
            flops=2 * half * syms * subs * k * c, bytes_accessed=2 * half * syms * subs * k, transcendentals=0
        ),
        name="kept",
    )(matrix, pilot_syms.reshape(1, -1), mod_order.reshape(1, -1), pilot_values, wave)
    return given, kept, facts, matrix


def entry(row, i):
    lane = lax.broadcasted_iota(jnp.int32, row.shape, 1)
    return jnp.sum(jnp.where(lane == i, row, 0.0), axis=1, keepdims=True)


def chosen_rows(chosen_ref, i, t, like):
    return jnp.broadcast_to(chosen_ref[i, t : t + 1, :], like.shape[-2:]) > 0.0


def as_column(row, count):
    diagonal = lax.broadcasted_iota(jnp.int32, (count, count), 0) == lax.broadcasted_iota(
        jnp.int32, (count, count), 1
    )
    return jnp.sum(jnp.where(diagonal, jnp.broadcast_to(row, (count, count)), 0.0), axis=1, keepdims=True)


def estimate_of(beams, pilot_re, pilot_im):
    c = beams.shape[-1]
    return beams * pilot_re + pltpu.roll(beams, c // 2, beams.ndim - 1) * pilot_im


def signed_pilots(pilot_ref, c):
    s = pilot_ref.shape[1]
    re = jnp.broadcast_to(as_column(pilot_ref[0:1, :], s), (s, c))
    im = jnp.broadcast_to(as_column(pilot_ref[1:2, :], s), (s, c))
    lane = lax.broadcasted_iota(jnp.int32, (s, c), 1)
    return re, jnp.where(lane < c // 2, im, -im)


def position():
    blocks = lax.axis_size(SUB)
    return lax.axis_index(PANEL) * blocks + lax.axis_index(SUB), lax.axis_size(PANEL) * blocks


def sum_kernel(chosen_ref, keep_ref, pilots_ref, parts_ref, *refs):
    *weights, own_ref, tail_ref, head_ref, llr_ref, patch_ref, wide_ref, even_ref, odd_ref = refs
    panels, syms, subs, c = parts_ref.shape

    def put(t, values):
        own_ref[t] = values
        head_ref[t] = values[:EDGE]
        tail_ref[t] = values[subs - EDGE :]

    at_pilots = [jnp.zeros((subs, c), jnp.float32) for _ in range(PILOTS)]
    for t in range(syms):
        total = parts_ref[0, t].astype(jnp.float32)
        for p in range(1, panels):
            total = total + parts_ref[p, t].astype(jnp.float32)
        beams = total.astype(jnp.bfloat16)
        put(t, beams)
        for i in range(PILOTS):
            at_pilots[i] = jnp.where(chosen_rows(chosen_ref, i, t, beams), beams.astype(jnp.float32), at_pilots[i])
    for i in range(PILOTS):
        put(syms + i, estimate_of(at_pilots[i], pilots_ref[0], pilots_ref[1]).astype(jnp.bfloat16))

    @pl.when(waits_long())
    def _():
        interior(chosen_ref, keep_ref, own_ref, *weights, llr_ref, patch_ref, wide_ref, even_ref, odd_ref)


def late_kernel(chosen_ref, keep_ref, own_ref, *refs):
    *weights, early_llr_ref, early_patch_ref, llr_ref, patch_ref, wide_ref, even_ref, odd_ref = refs
    del early_llr_ref, early_patch_ref

    @pl.when(jnp.logical_not(waits_long()))
    def _():
        interior(chosen_ref, keep_ref, own_ref, *weights, llr_ref, patch_ref, wide_ref, even_ref, odd_ref)


def waits_long():
    return lax.axis_index(SUB) < FIRST


def interior_shapes(syms, subs, c, layers, bits):
    return [
        jax.ShapeDtypeStruct((syms, subs, bits), jnp.float32),
        jax.ShapeDtypeStruct((layers - 1, syms, 2 * EDGE, c), jnp.float32),
    ]


def interior_scratch(syms, subs, c):
    padded = (syms + 2) * subs
    return [pltpu.VMEM((padded, lanes * c), jnp.bfloat16) for lanes in (2, 1, 1)]


def sum_beams(parts, facts, weights):
    _, syms, subs, c = parts.shape
    vmem = pl.BlockSpec(memory_space=pltpu.VMEM)
    edge = jax.ShapeDtypeStruct((syms + PILOTS, EDGE, c), jnp.bfloat16)
    layers, bits = weights[1].shape[0] + 1, weights[-1].shape[1]
    return pl.pallas_call(
        sum_kernel,
        in_specs=[vmem] * 10,
        out_specs=[vmem] * 5,
        out_shape=[
            jax.ShapeDtypeStruct((syms + PILOTS, subs, c), jnp.bfloat16),
            edge,
            edge,
            *interior_shapes(syms, subs, c, layers, bits),
        ],
        scratch_shapes=interior_scratch(syms, subs, c),
        compiler_params=pltpu.CompilerParams(vmem_limit_bytes=16 * 2**20),
        name="sum_beams",
    )(*facts, parts, *weights)


def pilot_rows(chosen_ref, rows, syms):
    spread = []
    for t in range(syms):
        row = jnp.zeros(rows.shape[1:], rows.dtype)
        for i in range(PILOTS):
            row = jnp.where(chosen_rows(chosen_ref, i, t, row), rows[i], row)
        spread.append(row)
    return jnp.stack(spread, 0)


def with_estimates(chosen_ref, pieces, syms):
    return jnp.concatenate([pieces[:syms], pilot_rows(chosen_ref, pieces[syms:], syms)], axis=2)


def taps_of(kernel, dt, dc):
    depth = kernel.shape[0] // 9
    return kernel[(3 * dt + dc) * depth : (3 * dt + dc + 1) * depth]


def demapped(field, in_ref, in_bias_ref, out_w_ref):
    hidden = jnp.dot(field, in_ref[...], preferred_element_type=jnp.float32)
    hidden = jnp.maximum(hidden + in_bias_ref[...], 0.0).astype(jnp.bfloat16)
    return jnp.dot(hidden, out_w_ref[...], preferred_element_type=jnp.float32)


def store_llr(ref, llr, keep, chosen_ref):
    rows = keep.shape[0]
    for t in range(ref.shape[0]):
        kept = keep > 0.0
        for i in range(PILOTS):
            kept = kept & jnp.logical_not(chosen_rows(chosen_ref, i, t, keep))
        ref[t] = jnp.where(kept, llr[t * rows : (t + 1) * rows], 0.0)


def interior(
    chosen_ref, keep_ref, own_ref, first_ref, rest_ref, bias_ref, in_ref, in_bias_ref, out_w_ref,
    llr_ref, patch_ref, wide_ref, even_ref, odd_ref,
):
    syms, subs, c = own_ref.shape
    syms = syms - PILOTS
    layers = rest_ref.shape[0] + 1
    rows = syms * subs
    for ref in (wide_ref, even_ref, odd_ref):
        ref[0:subs] = jnp.zeros((subs, ref.shape[1]), jnp.bfloat16)
        ref[subs + rows :] = jnp.zeros((subs, ref.shape[1]), jnp.bfloat16)
    wide_ref[subs : subs + rows, :c] = own_ref[:syms].reshape(rows, c)
    estimates = pilot_rows(chosen_ref, own_ref[syms:].astype(jnp.float32), syms)
    for t in range(syms):
        wide_ref[subs * (t + 1) : subs * (t + 2), c:] = estimates[t].astype(jnp.bfloat16)
    src = wide_ref
    for layer in range(1, layers + 1):
        kernel = first_ref[...] if layer == 1 else rest_ref[layer - 2]
        taps = jnp.concatenate([src[dt * subs : dt * subs + rows] for dt in range(3)], axis=1)
        wide = jnp.concatenate(
            [jnp.concatenate([taps_of(kernel, dt, dc) for dc in range(3)], axis=1) for dt in range(3)], axis=0
        )
        sums = jnp.dot(taps, wide, preferred_element_type=jnp.float32)
        total = sums[:, :c] + bias_ref[layer - 1 : layer, :]
        for dc in range(1, 3):
            total = total + pltpu.roll(sums[:, dc * c : (dc + 1) * c], rows - dc, 0)
        total = jnp.maximum(total, 0.0)
        if layer == layers:
            break
        src = (even_ref, odd_ref)[layer % 2]
        src[subs : subs + rows] = total.astype(jnp.bfloat16)
        spread = total.reshape(syms, subs, c)
        last = subs - 4 - 2 * layer
        group, place = last // EDGE * EDGE, last % EDGE
        high = spread[:, group : group + EDGE]
        if place != EDGE - 2:
            high = pltpu.roll(high, EDGE - 2 - place, 1)
        patch_ref[layer - 1] = jnp.concatenate([pltpu.roll(spread[:, :EDGE], EDGE - 2, 1), high], axis=1)
    final = pltpu.roll(total, layers, 0).astype(jnp.bfloat16)
    llr = demapped(final, in_ref, in_bias_ref, out_w_ref)
    store_llr(llr_ref, llr, keep_ref[...], chosen_ref)


def edge_kernel(
    chosen_ref, keep_ref, left_ref, right_ref, tail_ref, head_ref, patch_ref, inner_ref,
    first_ref, rest_ref, bias_ref, in_ref, in_bias_ref, out_w_ref,
    llr_ref, llr_buf, sems,
):
    syms, c = left_ref.shape[0] - PILOTS, left_ref.shape[2]
    layers = rest_ref.shape[0] + 1
    subs = llr_ref.shape[1]
    width = 2 * EDGE
    rows = syms * width
    middle = pl.ds(EDGE, subs - 2 * EDGE)
    inner_copy = pltpu.make_async_copy(inner_ref.at[:, middle], llr_ref.at[:, middle], sems.at[2])
    inner_copy.start()

    def joined(before, after, start):
        if start == 0:
            return before
        if start == EDGE:
            return after
        row = lax.broadcasted_iota(jnp.int32, before.shape, 1)
        turn = EDGE - start
        return jnp.where(row < turn, pltpu.roll(before, turn, 1), pltpu.roll(after, turn, 1))

    def convolved(shifted, kernel, bias):
        field = jnp.concatenate(shifted, axis=2)
        wide = jnp.concatenate(
            [jnp.concatenate([taps_of(kernel, dt, dc) for dt in range(3)], axis=1) for dc in range(3)], axis=0
        )
        sums = jnp.dot(
            field.reshape(syms * EDGE, field.shape[2]).astype(jnp.bfloat16), wide, preferred_element_type=jnp.float32
        ).reshape(syms, EDGE, 3 * c)
        nothing = jnp.zeros((1, EDGE, c), jnp.float32)
        total = sums[:, :, c : 2 * c] + bias[None]
        total = total + jnp.concatenate([nothing, sums[:-1, :, :c]], axis=0)
        total = total + jnp.concatenate([sums[1:, :, 2 * c :], nothing], axis=0)
        return jnp.maximum(total, 0.0)

    at, blocks = position()
    left, right, tail, head = (ref[...].astype(jnp.float32) for ref in (left_ref, right_ref, tail_ref, head_ref))
    fields = [
        [with_estimates(chosen_ref, joined(*ends, start + dc), syms) for dc in range(3)]
        for ends, start in (((left, head), EDGE - layers), ((tail, right), EDGE - 4))
    ]
    low, high = (convolved(field, first_ref[...], bias_ref[0:1, :]) for field in fields)
    row = lax.broadcasted_iota(jnp.int32, (EDGE, c), 0)
    for layer in range(1, layers):
        low = jnp.where(((row < layers - layer) & (at == 0))[None], 0.0, low)
        high = jnp.where(((row >= 2 + layer) & (at == blocks - 1))[None], 0.0, high)
        patch = patch_ref[layer - 1]
        fields = [
            [joined(low, patch[:, :EDGE], dc) for dc in range(3)],
            [joined(patch[:, EDGE:], high, EDGE - 2 + dc) for dc in range(3)],
        ]
        low, high = (convolved(field, rest_ref[layer - 1], bias_ref[layer : layer + 1, :]) for field in fields)
    total = jnp.concatenate([low, high], axis=1)
    llr = demapped(total.reshape(rows, c).astype(jnp.bfloat16), in_ref, in_bias_ref, out_w_ref)
    keep = jnp.concatenate([keep_ref[:EDGE], keep_ref[subs - EDGE :]], axis=0)
    store_llr(llr_buf, llr, keep, chosen_ref)
    copies = [
        pltpu.make_async_copy(
            llr_buf.at[:, pl.ds(side * EDGE, EDGE)], llr_ref.at[:, pl.ds(start, EDGE)], sems.at[side]
        )
        for side, start in enumerate((0, subs - EDGE))
    ]
    for copy in copies:
        copy.start()
    inner_copy.wait()
    for copy in copies:
        copy.wait()


def receive_interior(facts, own, weights, early):
    syms, subs, c = own.shape
    syms = syms - PILOTS
    layers, bits = weights[1].shape[0] + 1, weights[-1].shape[1]
    vmem = pl.BlockSpec(memory_space=pltpu.VMEM)
    return pl.pallas_call(
        late_kernel,
        in_specs=[vmem] * 11,
        out_specs=[vmem] * 2,
        out_shape=interior_shapes(syms, subs, c, layers, bits),
        input_output_aliases={9: 0, 10: 1},
        scratch_shapes=interior_scratch(syms, subs, c),
        compiler_params=pltpu.CompilerParams(vmem_limit_bytes=16 * 2**20),
        cost_estimate=pl.CostEstimate(flops=10**9, bytes_accessed=4 * 10**6, transcendentals=0),
        name="interior",
    )(*facts[:2], own, *weights, *early)


def receive_edges(facts, got, sent, patch, weights, inner):
    syms, subs, bits = inner.shape
    vmem = pl.BlockSpec(memory_space=pltpu.VMEM)
    return pl.pallas_call(
        edge_kernel,
        in_specs=[vmem] * 14,
        out_specs=pl.BlockSpec(memory_space=pltpu.HBM),
        out_shape=pltpu.HBM(inner.shape, jnp.float32),
        scratch_shapes=[
            pltpu.VMEM((syms, 2 * EDGE, bits), jnp.float32),
            pltpu.SemaphoreType.DMA((3,)),
        ],
        compiler_params=pltpu.CompilerParams(vmem_limit_bytes=16 * 2**20),
        cost_estimate=pl.CostEstimate(flops=5 * 10**8, bytes_accessed=4 * 10**6, transcendentals=0),
        name="edges",
    )(*facts[:2], *got, *sent, patch, inner, *weights)


def per_device(
    captured_waveform,
    element_lookup,
    combiner,
    pilot_syms,
    pilot_values,
    mod_order,
    conv_first,
    conv_rest,
    conv_bias,
    demap_in,
    demap_bias,
    demap_out,
):
    given, kept, facts, matrix = beam_partials(
        captured_waveform, element_lookup, combiner, pilot_syms, mod_order, pilot_values, demap_out.shape[1]
    )
    panels = lax.axis_size(PANEL)
    got = lax.ppermute(given, PANEL, [(p, p ^ 1) for p in range(panels)])
    pairs = pair_sums(matrix, kept, got, captured_waveform)
    same_core = [list(range(core, panels, 2)) for core in range(2)]
    parts = lax.all_to_all(pairs, PANEL, 0, 0, axis_index_groups=same_core, tiled=True)
    c = combiner.shape[1]
    weights = (
        conv_first.reshape(-1, c),
        conv_rest.reshape(conv_rest.shape[0], -1, c),
        conv_bias,
        demap_in,
        demap_bias.reshape(1, -1),
        demap_out,
    )
    own, tail, head, *early = sum_beams(parts, facts, weights)
    both = (PANEL, SUB)
    count = lax.axis_size(both)
    left = lax.ppermute(tail, both, [(i, i + 1) for i in range(count - 1)])
    right = lax.ppermute(head, both, [(i + 1, i) for i in range(count - 1)])
    inner, patch = receive_interior(facts, own, weights, early)
    return receive_edges(facts, (left, right), (tail, head), patch, weights, inner)


def solution(mesh):
    in_specs = (
        P(None, None, SUB, PANEL),
        P(PANEL),
        P(PANEL, None),
        P(),
        P(None, (PANEL, SUB)),
        P((PANEL, SUB)),
        P(),
        P(),
        P(),
        P(),
        P(),
        P(),
    )
    out_specs = P(None, (PANEL, SUB), None)
    return jax.shard_map(
        per_device, mesh=mesh, in_specs=in_specs, out_specs=out_specs, check_vma=False
    )
```
